256 devices in a mesh: seq: 32 (over y, z), dp: 8 (over x, core).
Axes of the slice: x: 4, y: 4, z: 8, core: 2. Of those that a mesh axis runs over, the one named last changes fastest.
Arguments:
- prefix: bfloat16 [8, 4096, 1024], P('dp', 'seq'), may hold values from -6 to 6
- latents: bfloat16 [8, 1024, 1024], P('dp', 'seq'), may hold values from -96 to 96
- saved_out: bfloat16 [8, 1024, 1024], P('dp', 'seq'), may hold values from -6 to 6
- out_grad: bfloat16 [8, 1024, 1024], P('dp', 'seq'), may hold values from -24 to 24
- visible: int32 [8, 1024], P('dp'), may hold values from 1 to 4096, as said below
- w_query: bfloat16 [1024, 1024], replicated, may hold values from -0.5625 to 0.5625
- w_key: bfloat16 [1024, 1024], replicated, may hold values from -0.5625 to 0.5625
- w_value: bfloat16 [1024, 1024], replicated, may hold values from -0.1875 to 0.1875
Outputs:
- prefix_grad: bfloat16 [8, 4096, 1024], P('dp', 'seq')
- latent_grad: bfloat16 [8, 1024, 1024], P('dp', 'seq')
- key_wgrad: float32 [1024, 1024], P(('seq', 'dp'))
The draws below stay inside these ranges and needn't reach their ends.
Inputs may be any that keep to these rules, and one draw needn't show every extreme that they name: Within a sample the visible lengths never fall from one latent to the next, and the last latent of every sample sees all 4096 prefix tokens.
All inputs are finite; a program needn't handle non-finite values.
Results may differ from the reference program's by a relative error of at most 0.022.
The reference program's roundings to bfloat16 on the way (of `probs_b`, `dscores`, `dq_block` and `dqueries_b`) count: a program that leaves them out, or rounds other values in their place, can miss the bound.
Values may be sent and summed in bfloat16 or wider, within the bound.
No kernel may reach another device: no remote copies, remote signals or barrier semaphores. Data moves between devices by JAX's collectives and lax.ppermute only.
A program may use at most 64 MiB of HBM per device.

```python
import math
import jax
import jax.numpy as jnp
from jax import lax

D = 1024
H = 16
LATENTS = 1024
PREFIX_DEV = 128
DH = 64
PREFIX = 4096
BATCH = 8
N_SEQ = 32


def draw_latents(key, part):
    key = jax.random.fold_in(key, 11)
    base = jax.random.truncated_normal(key, -6.0, 6.0, (BATCH, LATENTS, D), jnp.float32)
    return base.astype(jnp.bfloat16)


def projection(key, factor):
    base = jax.random.truncated_normal(key, -6.0, 6.0, (D, D), jnp.float32)
    return (base * (factor / math.sqrt(D))).astype(jnp.bfloat16)


def draw_w_query(key, part):
    key = jax.random.fold_in(key, 12)
    return projection(key, 1.0)


def draw_w_key(key, part):
    key = jax.random.fold_in(key, 13)
    return projection(key, 1.0)


def draw_visible(key, part):
    key = jax.random.fold_in(key, 14)
    counts = jax.random.randint(key, (BATCH, LATENTS), 1, PREFIX + 1, dtype=jnp.int32)
    counts = jnp.sort(counts, axis=1)
    return counts.at[:, LATENTS - 1].set(PREFIX)


def with_spikes(values, own_key, source, target, shards_of, factor):
    def block_of(axis_at):
        return (jnp.arange(values.shape[axis_at]) // (values.shape[axis_at] // shards_of)).reshape((-1,) + (1,) * (values.ndim - 1 - axis_at))

    one_side = jax.random.permutation(own_key, shards_of)[block_of(target)]
    far = (block_of(target) + shards_of // 2) % shards_of
    return jnp.where((block_of(source) == one_side) | (block_of(source) == far), factor * values, values)


def levels(key, extent, cuts, smallest, largest):
    def one(axis_at, shards_of):
        draws = jax.random.uniform(jax.random.fold_in(jax.random.fold_in(key, 6), axis_at), (shards_of,), jnp.float32, smallest / len(cuts), largest / len(cuts))
        return jnp.repeat(jnp.exp(draws), extent[axis_at] // shards_of).reshape((-1,) + (1,) * (len(extent) - axis_at - 1))

    gain = one(*cuts[0])
    for cut in cuts[1:]:
        gain = gain * one(*cut)
    return gain


def scatter_about(own_key, extent, width, limit, pieces=(), held_as=jnp.bfloat16):
    result = width * jax.random.normal(own_key, extent, jnp.float32)
    if pieces:
        result = result * levels(own_key, extent, pieces, -0.22, 0.18)
    return jnp.clip(result, -limit, limit).astype(held_as)


def heavy_noise(stream_key, extent, spread, reach, cuts, heavy, kind=jnp.bfloat16):
    drawn = spread * jax.random.normal(stream_key, extent, jnp.float32)
    if cuts:
        drawn = drawn * levels(stream_key, extent, cuts, -0.22, 0.18)
    return jnp.clip(with_spikes(drawn, jax.random.fold_in(stream_key, 3), *heavy), -reach, reach).astype(kind)


def setup_inputs(seed: int = 0) -> dict:
    key_list = jax.random.split(jax.random.key(seed), 9)
    prefix = heavy_noise(key_list[0], (BATCH, PREFIX, D), 1.0, 6.0, ((0, 8), (1, 32)), (1, 2, 32, 2.75))
    latents = draw_latents(jax.random.fold_in(key_list[8], 71), 0)
    saved_out = scatter_about(key_list[2], (BATCH, LATENTS, D), 1.0, 6.0, ((0, 8), (1, 32)))
    out_grad = scatter_about(key_list[3], (BATCH, LATENTS, D), 4.0, 24.0, ((0, 8), (1, 32)))
    visible = draw_visible(jax.random.fold_in(key_list[8], 71), 0)
    w_query = draw_w_query(jax.random.fold_in(key_list[8], 71), 0)
    w_key = draw_w_key(jax.random.fold_in(key_list[8], 71), 0)
    w_value = scatter_about(key_list[7], (D, D), D ** -0.5, 0.1875)
    return {"prefix": prefix, "latents": latents, "saved_out": saved_out, "out_grad": out_grad, "visible": visible, "w_query": w_query, "w_key": w_key, "w_value": w_value}


def sample_grads(prefix, latents, saved_out, out_grad, visible, w_query, w_key, w_value):
    scale = 1.0 / math.sqrt(DH)
    queries = jnp.dot(latents, w_query, preferred_element_type=jnp.float32).astype(jnp.bfloat16)
    keys = jnp.dot(prefix, w_key, preferred_element_type=jnp.float32).astype(jnp.bfloat16)
    values = jnp.dot(prefix, w_value, preferred_element_type=jnp.float32).astype(jnp.bfloat16)
    mask = jnp.arange(PREFIX, dtype=jnp.int32)[None, :] < visible[:, None]
    delta = (out_grad.astype(jnp.float32) * saved_out.astype(jnp.float32)).reshape(LATENTS, H, DH).sum(-1)

    def one_head(head):
        offset = (head * DH).astype(jnp.int32)
        q_head = lax.dynamic_slice_in_dim(queries, offset, DH, 1)
        k_head = lax.dynamic_slice_in_dim(keys, offset, DH, 1)
        v_head = lax.dynamic_slice_in_dim(values, offset, DH, 1)
        g_head = lax.dynamic_slice_in_dim(out_grad, offset, DH, 1)
        d_head = lax.dynamic_index_in_dim(delta, head.astype(jnp.int32), 1, keepdims=False)
        scores = jnp.dot(q_head, k_head.T, preferred_element_type=jnp.float32) * scale
        scores = jnp.where(mask, scores, jnp.float32(-1e+30))
        rowmax = lax.optimization_barrier(jnp.max(scores, axis=1))
        total = lax.optimization_barrier(jnp.sum(jnp.where(mask, jnp.exp(scores - rowmax[:, None]), jnp.float32(0.0)), axis=1))
        lse = rowmax + jnp.log(total)
        probs = jnp.where(mask, jnp.exp(scores - lse[:, None]), jnp.float32(0.0))
        probs_b = probs.astype(jnp.bfloat16)
        dprobs = jnp.dot(g_head, v_head.T, preferred_element_type=jnp.float32)
        dscores = (probs * (dprobs - d_head[:, None]) * scale).astype(jnp.bfloat16)
        dvalues = jnp.dot(probs_b.T, g_head, preferred_element_type=jnp.float32).astype(jnp.bfloat16)
        dkeys = jnp.dot(dscores.T, q_head, preferred_element_type=jnp.float32).astype(jnp.bfloat16)
        score_blocks = dscores.reshape(LATENTS, N_SEQ, PREFIX_DEV).astype(jnp.float32)
        key_blocks = k_head.reshape(N_SEQ, PREFIX_DEV, DH).astype(jnp.float32)
        dq_block = jnp.einsum('isp,spd->sid', score_blocks, key_blocks).astype(jnp.bfloat16)
        dqueries = lax.optimization_barrier(jnp.sum(dq_block.astype(jnp.float32), axis=0))
        return (dqueries, dkeys, dvalues)
    dqueries, dkeys, dvalues = lax.map(one_head, jnp.arange(H, dtype=jnp.int32))
    dqueries = dqueries.transpose(1, 0, 2).reshape(LATENTS, D)
    dkeys = dkeys.transpose(1, 0, 2).reshape(PREFIX, D)
    dvalues = dvalues.transpose(1, 0, 2).reshape(PREFIX, D)
    dqueries_b = dqueries.astype(jnp.bfloat16)
    latent_grad = jnp.dot(dqueries_b, w_query.T, preferred_element_type=jnp.float32).astype(jnp.bfloat16)
    prefix_grad = (jnp.dot(dkeys, w_key.T, preferred_element_type=jnp.float32) + jnp.dot(dvalues, w_value.T, preferred_element_type=jnp.float32)).astype(jnp.bfloat16)
    key_part = jnp.dot(prefix.T, dkeys, preferred_element_type=jnp.float32)
    return (prefix_grad, latent_grad, key_part)

def reference(prefix, latents, saved_out, out_grad, visible, w_query, w_key, w_value):

    def per_sample(index):
        return sample_grads(prefix[index], latents[index], saved_out[index], out_grad[index], visible[index], w_query, w_key, w_value)
    prefix_grad, latent_grad, key_part = lax.map(per_sample, jnp.arange(BATCH, dtype=jnp.int32))
    return (prefix_grad, latent_grad, lax.optimization_barrier(jnp.sum(key_part, axis=0)))
```

```python
import functools
import math

import jax
import jax.numpy as jnp
from jax import lax
from jax.experimental import pallas as pl
from jax.experimental.pallas import tpu as pltpu
from jax.sharding import Mesh, PartitionSpec as P

BF = jnp.bfloat16
F32 = jnp.float32
DH = 64
NEG = -1e30
FLOOR = -1e29
SCALE = 1.0 / math.sqrt(DH)
C = SCALE * math.log2(math.e)
NT_DIMS = (((1,), (1,)), ((), ()))
VMEM_LIMIT = 48 * 1024 * 1024
LAT_TILE = 256
SRC_CHUNK = 8


def dot(a, b):
    return jnp.dot(a, b, preferred_element_type=F32)


def dot_nt(a, b):
    return lax.dot_general(a, b, NT_DIMS, preferred_element_type=F32)


def swap(x):
    return jnp.concatenate([x[..., 64:], x[..., :64]], axis=-1)


def fold(x, rows):
    return jnp.concatenate([x[:rows], x[rows:]], axis=1)


def pre_kernel(prefix, latents, grad, saved, w_query, w_key, w_value, kq, vg):
    keys = dot(prefix[...], w_key[...]).astype(BF)
    values = dot(prefix[...], w_value[...]).astype(BF)
    queries = dot(latents[...], w_query[...]).astype(BF)
    g = grad[...]
    product = g.astype(F32) * saved[...].astype(F32)
    lat = product.shape[0]
    product = jnp.concatenate([product, jnp.zeros((128 - lat, product.shape[1]), F32)], axis=0)
    product = product.T
    half_tok = prefix.shape[0] // 2
    for head in range(4):
        cols = slice(head * DH, (head + 1) * DH)
        delta = jnp.sum(product[cols], axis=0, keepdims=True)
        high = delta.astype(BF)
        rest = delta - high.astype(F32)
        mid = rest.astype(BF)
        low = (rest - mid.astype(F32)).astype(BF)
        row = lax.broadcasted_iota(jnp.int32, (16, 128), 0)
        parts = jnp.where(
            row == 0,
            high.astype(F32),
            jnp.where(row == 1, mid.astype(F32), jnp.where(row == 2, low.astype(F32), 0.0)),
        ).astype(BF)
        q_fold = fold(queries[:, cols], lat // 2)
        g_fold = fold(g[:, cols], lat // 2)
        for half in range(2):
            toks = slice(half * half_tok, (half + 1) * half_tok)
            dest = 2 * head + half
            kq[dest, 0:32, :] = fold(keys[toks, cols], half_tok // 2)
            kq[dest, 32:48, :] = q_fold
            vg[dest, 0:32, :] = fold(values[toks, cols], half_tok // 2)
            vg[dest, 32:48, :] = g_fold
            vg[dest, 48:64, :] = parts


def unfold(folded, low_ref, high_ref):
    lane = lax.broadcasted_iota(jnp.int32, folded.shape, 2)
    other = swap(folded)
    zero = jnp.zeros_like(folded)
    left = lane < 64
    low = jnp.concatenate([jnp.where(left, folded, zero), jnp.where(left, other, zero)], axis=1)
    high = jnp.concatenate([jnp.where(left, zero, other), jnp.where(left, zero, folded)], axis=1)
    low_ref[...] = low.reshape(low_ref.shape)
    high_ref[...] = high.reshape(high_ref.shape)


def chunk_tokens(chunk, half, rows, cols):
    row = lax.broadcasted_iota(jnp.int32, (rows, cols), 0)
    return (chunk * SRC_CHUNK + (row >> 5)) * 128 + half * 64 + (row & 31)


def chunk_count(vis_s, half, tile):
    span = SRC_CHUNK * 128
    seen = vis_s[(tile + 1) * LAT_TILE - 1] - half * 64
    seen = jnp.maximum(seen, 0)
    return jnp.minimum((seen + span - 1) // span, 32 // SRC_CHUNK)


def stats_kernel(vis_s, half_s, vis, kq, out, q_low, q_high):
    half = half_s[0]
    unfold(kq[:, 32:48, :], q_low, q_high)
    rows = SRC_CHUNK * 32
    for tile in range(1024 // LAT_TILE):
        lanes = slice(tile * LAT_TILE, (tile + 1) * LAT_TILE)
        seen = vis[:, lanes]
        ql = q_low[lanes, :]
        qh = q_high[lanes, :]

        def step(chunk, carry):
            top, total = carry
            k = kq[pl.ds(chunk * SRC_CHUNK, SRC_CHUNK), 0:32, :].reshape(rows, 128)
            tok = chunk_tokens(chunk, half, rows, LAT_TILE)
            s_low = jnp.where(tok < seen, dot_nt(k, ql), NEG)
            s_high = jnp.where(tok < seen - 32, dot_nt(k, qh), NEG)
            new = jnp.maximum(jnp.max(s_low, axis=0, keepdims=True), jnp.max(s_high, axis=0, keepdims=True))
            new = jnp.maximum(new, top)
            part = jnp.sum(jnp.exp2((s_low - new) * C), axis=0, keepdims=True) + jnp.sum(
                jnp.exp2((s_high - new) * C), axis=0, keepdims=True
            )
            return new, total * jnp.exp2((top - new) * C) + part

        start = (jnp.full((1, LAT_TILE), FLOOR, F32), jnp.zeros((1, LAT_TILE), F32))
        top, total = lax.fori_loop(0, chunk_count(vis_s, half, tile), step, start)
        out[0:1, lanes] = top
        out[1:2, lanes] = total
    out[2:8, :] = jnp.zeros((6, 1024), F32)


def grad_kernel(vis_s, half_s, vis, kq, vg, own, other, dk_out, dvq_out,
                q_low, q_high, g_low, g_high, k_t, dk_acc, dv_acc, delta_ref):
    half = half_s[0]
    rows = SRC_CHUNK * 32
    unfold(kq[:, 32:48, :], q_low, q_high)
    unfold(vg[:, 32:48, :], g_low, g_high)
    for chunk in range(32 // SRC_CHUNK):
        k = kq[chunk * SRC_CHUNK : (chunk + 1) * SRC_CHUNK, 0:32, :].reshape(rows, 128)
        turned = k.T
        k_t[chunk] = jnp.concatenate([turned[0:64], turned[64:128]], axis=1)
    dk_acc[...] = jnp.zeros_like(dk_acc)
    dv_acc[...] = jnp.zeros_like(dv_acc)
    lane = lax.broadcasted_iota(jnp.int32, (1, 128), 1)
    for block in range(8):
        joined = jnp.zeros((1, 128), F32)
        for place in range(4):
            parts = vg[4 * block + place, 48:64, :].astype(F32)
            parts = jnp.sum(parts, axis=0, keepdims=True)
            if place:
                parts = pltpu.roll(parts, 32 * place, 1)
            joined = jnp.where((lane >> 5) == place, parts, joined)
        delta_ref[:, block * 128 : (block + 1) * 128] = joined
    top = jnp.maximum(own[0:1, :], other[0:1, :])
    total = own[1:2, :] * jnp.exp2((own[0:1, :] - top) * C) + other[1:2, :] * jnp.exp2((other[0:1, :] - top) * C)
    lse = top + jnp.log2(total) * (1.0 / C)
    for tile in range(1024 // LAT_TILE):
        lanes = slice(tile * LAT_TILE, (tile + 1) * LAT_TILE)
        seen = vis[:, lanes]
        lse_t = lse[:, lanes]
        delta = delta_ref[:, lanes]
        ql, qh, gl, gh = q_low[lanes, :], q_high[lanes, :], g_low[lanes, :], g_high[lanes, :]

        def step(chunk, dq):
            srcs = pl.ds(chunk * SRC_CHUNK, SRC_CHUNK)
            k = kq[srcs, 0:32, :].reshape(rows, 128)
            v = vg[srcs, 0:32, :].reshape(rows, 128)
            tok = chunk_tokens(chunk, half, rows, LAT_TILE)
            p_low = jnp.exp2((jnp.where(tok < seen, dot_nt(k, ql), NEG) - lse_t) * C)
            p_high = jnp.exp2((jnp.where(tok < seen - 32, dot_nt(k, qh), NEG) - lse_t) * C)
            ds_low = (p_low * (dot_nt(v, gl) - delta)).astype(BF)
            ds_high = (p_high * (dot_nt(v, gh) - delta)).astype(BF)
            place = pl.ds(pl.multiple_of(chunk * rows, rows), rows)
            dv_acc[place, :] += dot(p_low.astype(BF), gl) + dot(p_high.astype(BF), gh)
            dk_acc[place, :] += dot(ds_low, ql) + dot(ds_high, qh)
            return dq + dot(k_t[chunk], jnp.concatenate([ds_low, ds_high], axis=0))

        dq = lax.fori_loop(0, chunk_count(vis_s, half, tile), step, jnp.zeros((DH, LAT_TILE), F32))
        dq = (dq * SCALE).T
        for block in range(LAT_TILE // 32):
            part = dq[block * 32 : (block + 1) * 32]
            dvq_out[tile * (LAT_TILE // 32) + block, 32:48, :] = fold(part, 16).astype(BF)
    dk_out[...] = (dk_acc[...] * SCALE).astype(BF).reshape(dk_out.shape)
    dvq_out[:, 0:32, :] = dv_acc[...].astype(BF).reshape(32, 32, 128)


def tokens_of(ref, half, side):
    pieces = []
    for head in range(16):
        pieces.append(ref[2 * head + half, 0:32, side * 64 : (side + 1) * 64])
    return jnp.concatenate(pieces, axis=1)


def join_kernel(folded, out):
    for half in range(2):
        for side in range(2):
            at = half * 64 + side * 32
            out[at : at + 32, :] = tokens_of(folded, half, side)


def key_kernel(own_t, other_t, own_dk, other_dk, out):
    part = dot(own_t[...], own_dk[...]) + dot(other_t[...], other_dk[...])
    out[...] = part.astype(BF).reshape(out.shape)


def post_kernel(dk, folded, w_query, w_key, w_value, prefix_grad, latent_grad, dv, dq):
    @pl.when(pl.program_id(0) == 0)
    def _():
        for half in range(2):
            for side in range(2):
                at = half * 64 + side * 32
                dv[at : at + 32, :] = tokens_of(folded, half, side)
        for side in range(2):
            pieces = []
            for head in range(16):
                part = [folded[2 * head + half, 32:48, side * 64 : (side + 1) * 64].astype(F32) for half in range(2)]
                pieces.append(part[0] + part[1])
            dq[side * 16 : (side + 1) * 16, :] = jnp.concatenate(pieces, axis=1).astype(BF)

    prefix_grad[...] = (dot_nt(dk[...], w_key[...]) + dot_nt(dv[...], w_value[...])).astype(BF)
    latent_grad[...] = dot_nt(dq[...], w_query[...]).astype(BF)


def call(kernel, out_shape, flops=0, nbytes=0, **kwargs):
    return pl.pallas_call(
        kernel,
        out_shape=out_shape,
        compiler_params=pltpu.CompilerParams(vmem_limit_bytes=VMEM_LIMIT),
        cost_estimate=pl.CostEstimate(flops=flops, bytes_accessed=nbytes, transcendentals=0),
        **kwargs,
    )


def on_device(prefix, latents, saved, grad, visible, w_query, w_key, w_value):
    prefix, latents, saved, grad = prefix[0], latents[0], saved[0], grad[0]
    vis_row = visible
    vis_flat = visible[0]
    half = jnp.reshape(lax.axis_index("z") % 2, (1,)).astype(jnp.int32)
    core = lax.axis_index("core")
    vmem = pl.BlockSpec(memory_space=pltpu.VMEM)
    smem = pl.BlockSpec(memory_space=pltpu.SMEM)
    shape = jax.ShapeDtypeStruct

    whole = lambda rows: pl.BlockSpec((rows, 1024), lambda i: (0, 0))
    cols = lambda rows: pl.BlockSpec((rows, 256), lambda i: (0, i))
    kq, vg = call(
        pre_kernel,
        (shape((32, 48, 128), BF), shape((32, 64, 128), BF)),
        flops=2 * 288 * 1024 * 1024,
        nbytes=8 << 20,
        grid=(4,),
        in_specs=[whole(128), whole(32), cols(32), cols(32), cols(1024), cols(1024), cols(1024)],
        out_specs=(
            pl.BlockSpec((8, 48, 128), lambda i: (i, 0, 0)),
            pl.BlockSpec((8, 64, 128), lambda i: (i, 0, 0)),
        ),
    )(prefix, latents, grad, saved, w_query, w_key, w_value)
    kq = lax.all_to_all(kq, ("y", "z"), 0, 0, tiled=True)
    vg = lax.all_to_all(vg, ("y", "z"), 0, 0, tiled=True)

    at = lax.broadcasted_iota(jnp.int32, (1024, 1024), 0)
    c_at, y_at, x_at, z_at, k_at = at >> 9, (at >> 7) & 3, (at >> 5) & 3, (at >> 2) & 7, at & 3
    c_at = jnp.where(core == 0, c_at, 1 - c_at)
    wanted = (y_at * 8 + z_at) * 32 + x_at * 8 + c_at * 4 + k_at
    pick = (wanted == lax.broadcasted_iota(jnp.int32, (1024, 1024), 1)).astype(BF)
    prefix_t = dot_nt(pick, prefix).astype(BF)
    own_t = prefix_t[:512]
    other_t = lax.ppermute(prefix_t[512:], "core", [(0, 1), (1, 0)])

    stats = call(
        stats_kernel,
        shape((8, 1024), F32),
        flops=2 * 1024 * 2048 * 64,
        nbytes=1 << 19,
        in_specs=[smem, smem, vmem, vmem],
        out_specs=vmem,
        scratch_shapes=[pltpu.VMEM((1024, 128), BF)] * 2,
    )(vis_flat, half, vis_row, kq)
    other = lax.ppermute(stats, "z", [(i, i ^ 1) for i in range(8)])
    dk_fold, dvq = call(
        grad_kernel,
        (shape((32, 32, 128), BF), shape((32, 48, 128), BF)),
        flops=10 * 1024 * 2048 * 64,
        nbytes=1 << 20,
        in_specs=[smem, smem] + [vmem] * 5,
        out_specs=(vmem, vmem),
        scratch_shapes=[pltpu.VMEM((1024, 128), BF)] * 4
        + [
            pltpu.VMEM((32 // SRC_CHUNK, DH, SRC_CHUNK * 64), BF),
            pltpu.VMEM((1024, 128), F32),
            pltpu.VMEM((1024, 128), F32),
            pltpu.VMEM((1, 1024), F32),
        ],
    )(vis_flat, half, vis_row, kq, vg, stats, other)
    dk_fold = lax.all_to_all(dk_fold, ("y", "z"), 0, 0, tiled=True)
    dvq = lax.all_to_all(dvq, ("y", "z"), 0, 0, tiled=True)

    dk = call(
        join_kernel,
        shape((128, 1024), BF),
        nbytes=1 << 19,
        in_specs=[vmem],
        out_specs=vmem,
    )(dk_fold)
    dk_other = lax.ppermute(dk, "core", [(0, 1), (1, 0)])
    part = call(
        key_kernel,
        shape((16, 32, 1024), BF),
        flops=2 * 512 * 256 * 1024,
        nbytes=2 << 20,
        in_specs=[vmem] * 4,
        out_specs=vmem,
    )(own_t, other_t, dk, dk_other)
    part = lax.all_to_all(part, ("y", "x"), 0, 0, tiled=True)
    part = jnp.sum(part.astype(F32), axis=0)
    part = lax.all_to_all(part.reshape(8, 4, 1024), "z", 0, 0, tiled=True)
    key_wgrad = jnp.sum(part, axis=0)

    rows = lambda n: pl.BlockSpec((256, 1024), lambda i: (i, 0))
    prefix_grad, latent_grad = call(
        post_kernel,
        (shape((128, 1024), BF), shape((32, 1024), BF)),
        flops=2 * 288 * 1024 * 1024,
        nbytes=8 << 20,
        grid=(4,),
        in_specs=[whole(128), pl.BlockSpec((32, 48, 128), lambda i: (0, 0, 0))] + [rows(256)] * 3,
        out_specs=(cols(128), cols(32)),
        scratch_shapes=[pltpu.VMEM((128, 1024), BF), pltpu.VMEM((32, 1024), BF)],
    )(dk, dvq, w_query, w_key, w_value)
    return prefix_grad[None], latent_grad[None], key_wgrad


def solution(mesh):
    grid = Mesh(mesh.devices.reshape(4, 8, 4, 2), ("y", "z", "x", "core"))
    seq, dp = ("y", "z"), ("x", "core")
    return jax.shard_map(
        on_device,
        mesh=grid,
        in_specs=(
            P(dp, seq, None),
            P(dp, seq, None),
            P(dp, seq, None),
            P(dp, seq, None),
            P(dp, None),
            P(),
            P(),
            P(),
        ),
        out_specs=(P(dp, seq, None), P(dp, seq, None), P(seq + dp, None)),
        check_vma=False,
    )
```

```python
import functools
import math

import jax
import jax.numpy as jnp
from jax import lax
from jax.experimental import pallas as pl
from jax.experimental.pallas import tpu as pltpu
from jax.sharding import Mesh, PartitionSpec as P

BF = jnp.bfloat16
F32 = jnp.float32
DH = 64
NEG = -1e30
FLOOR = -1e29
SCALE = 1.0 / math.sqrt(DH)
C = SCALE * math.log2(math.e)
NT_DIMS = (((1,), (1,)), ((), ()))
LAT_TILE = 256
SRC_CHUNK = 8


def dot(a, b):
    return jnp.dot(a, b, preferred_element_type=F32)


def dot_nt(a, b):
    return lax.dot_general(a, b, NT_DIMS, preferred_element_type=F32)


def swap(x):
    return jnp.concatenate([x[..., 64:], x[..., :64]], axis=-1)


def fold(x, rows):
    return jnp.concatenate([x[:rows], x[rows:]], axis=1)


def pre_kernel(prefix, latents, grad, saved, w_query, w_key, w_value, out):
    keys = dot(prefix[...], w_key[...]).astype(BF)
    values = dot(prefix[...], w_value[...]).astype(BF)
    queries = dot(latents[...], w_query[...]).astype(BF)
    g = grad[...]
    product = g.astype(F32) * saved[...].astype(F32)
    product = jnp.concatenate([product, jnp.zeros((96, product.shape[1]), F32)], axis=0).T
    row = lax.broadcasted_iota(jnp.int32, (8, 128), 0)
    for head in range(4):
        cols = slice(head * DH, (head + 1) * DH)
        delta = jnp.sum(product[cols], axis=0, keepdims=True)
        high = delta.astype(BF).astype(F32)
        mid = (delta - high).astype(BF).astype(F32)
        low = delta - high - mid
        parts = jnp.where(row == 0, high, jnp.where(row == 1, mid, jnp.where(row == 2, low, 0.0)))
        q_fold = fold(queries[:, cols], 16)
        g_fold = fold(g[:, cols], 16)
        for half in range(2):
            toks = slice(half * 64, (half + 1) * 64)
            dest = 2 * head + half
            out[dest, 0:32, :] = fold(keys[toks, cols], 32)
            out[dest, 32:64, :] = fold(values[toks, cols], 32)
            out[dest, 64:80, :] = q_fold
            out[dest, 80:96, :] = g_fold
            out[dest, 96:104, :] = parts.astype(BF)


def unfold(folded, low_ref, high_ref):
    lane = lax.broadcasted_iota(jnp.int32, folded.shape, 2)
    other = swap(folded)
    zero = jnp.zeros_like(folded)
    left = lane < 64
    low = jnp.concatenate([jnp.where(left, folded, zero), jnp.where(left, other, zero)], axis=1)
    high = jnp.concatenate([jnp.where(left, zero, other), jnp.where(left, zero, folded)], axis=1)
    low_ref[...] = low.reshape(low_ref.shape)
    high_ref[...] = high.reshape(high_ref.shape)


def chunk_tokens(chunk, half, rows, cols):
    row = lax.broadcasted_iota(jnp.int32, (rows, cols), 0)
    return (chunk * SRC_CHUNK + (row >> 5)) * 128 + half * 64 + (row & 31)


def chunk_count(vis_s, half, tile):
    span = SRC_CHUNK * 128
    seen = vis_s[(tile + 1) * LAT_TILE - 1] - half * 64
    seen = jnp.maximum(seen, 0)
    return jnp.minimum((seen + span - 1) // span, 32 // SRC_CHUNK)


def stats_kernel(vis_s, half_s, vis, data, out, q_low, q_high):
    half = half_s[0]
    unfold(data[:, 64:80, :], q_low, q_high)
    rows = SRC_CHUNK * 32
    for tile in range(1024 // LAT_TILE):
        lanes = slice(tile * LAT_TILE, (tile + 1) * LAT_TILE)
        seen = vis[:, lanes]
        ql = q_low[lanes, :]
        qh = q_high[lanes, :]

        def step(chunk, carry):
            top, total = carry
            k = data[pl.ds(chunk * SRC_CHUNK, SRC_CHUNK), 0:32, :].reshape(rows, 128)
            tok = chunk_tokens(chunk, half, rows, LAT_TILE)
            s_low = jnp.where(tok < seen, dot_nt(k, ql), NEG)
            s_high = jnp.where(tok < seen - 32, dot_nt(k, qh), NEG)
            new = jnp.maximum(jnp.max(s_low, axis=0, keepdims=True), jnp.max(s_high, axis=0, keepdims=True))
            new = jnp.maximum(new, top)
            part = jnp.sum(jnp.exp2((s_low - new) * C), axis=0, keepdims=True) + jnp.sum(
                jnp.exp2((s_high - new) * C), axis=0, keepdims=True
            )
            return new, total * jnp.exp2((top - new) * C) + part

        start = (jnp.full((1, LAT_TILE), FLOOR, F32), jnp.zeros((1, LAT_TILE), F32))
        top, total = lax.fori_loop(0, chunk_count(vis_s, half, tile), step, start)
        out[0:1, lanes] = top
        out[1:2, lanes] = total
    out[2:8, :] = jnp.zeros((6, 1024), F32)


def grad_kernel(vis_s, half_s, vis, data, own, other, out,
                q_low, q_high, g_low, g_high, k_t, dk_acc, dv_acc, delta_ref):
    half = half_s[0]
    rows = SRC_CHUNK * 32
    unfold(data[:, 64:80, :], q_low, q_high)
    unfold(data[:, 80:96, :], g_low, g_high)
    for chunk in range(32 // SRC_CHUNK):
        k = data[chunk * SRC_CHUNK : (chunk + 1) * SRC_CHUNK, 0:32, :].reshape(rows, 128)
        turned = k.T
        k_t[chunk] = jnp.concatenate([turned[0:64], turned[64:128]], axis=1)
    dk_acc[...] = jnp.zeros_like(dk_acc)
    dv_acc[...] = jnp.zeros_like(dv_acc)
    lane = lax.broadcasted_iota(jnp.int32, (1, 128), 1)
    for block in range(8):
        joined = jnp.zeros((1, 128), F32)
        for place in range(4):
            parts = data[4 * block + place, 96:104, :].astype(F32)
            parts = jnp.sum(parts, axis=0, keepdims=True)
            if place:
                parts = pltpu.roll(parts, 32 * place, 1)
            joined = jnp.where((lane >> 5) == place, parts, joined)
        delta_ref[:, block * 128 : (block + 1) * 128] = joined
    top = jnp.maximum(own[0:1, :], other[0:1, :])
    total = own[1:2, :] * jnp.exp2((own[0:1, :] - top) * C) + other[1:2, :] * jnp.exp2((other[0:1, :] - top) * C)
    lse = top + jnp.log2(total) * (1.0 / C)
    for tile in range(1024 // LAT_TILE):
        lanes = slice(tile * LAT_TILE, (tile + 1) * LAT_TILE)
        seen = vis[:, lanes]
        lse_t = lse[:, lanes]
        delta = delta_ref[:, lanes]
        ql, qh, gl, gh = q_low[lanes, :], q_high[lanes, :], g_low[lanes, :], g_high[lanes, :]

        def step(chunk, dq):
            srcs = pl.ds(chunk * SRC_CHUNK, SRC_CHUNK)
            k = data[srcs, 0:32, :].reshape(rows, 128)
            v = data[srcs, 32:64, :].reshape(rows, 128)
            tok = chunk_tokens(chunk, half, rows, LAT_TILE)
            p_low = jnp.exp2((jnp.where(tok < seen, dot_nt(k, ql), NEG) - lse_t) * C)
            p_high = jnp.exp2((jnp.where(tok < seen - 32, dot_nt(k, qh), NEG) - lse_t) * C)
            ds_low = (p_low * (dot_nt(v, gl) - delta)).astype(BF)
            ds_high = (p_high * (dot_nt(v, gh) - delta)).astype(BF)
            place = pl.ds(pl.multiple_of(chunk * rows, rows), rows)
            dv_acc[place, :] += dot(p_low.astype(BF), gl) + dot(p_high.astype(BF), gh)
            dk_acc[place, :] += dot(ds_low, ql) + dot(ds_high, qh)
            return dq + dot(k_t[chunk], jnp.concatenate([ds_low, ds_high], axis=0))

        dq = lax.fori_loop(0, chunk_count(vis_s, half, tile), step, jnp.zeros((DH, LAT_TILE), F32))
        dq = (dq * SCALE).T
        for block in range(LAT_TILE // 32):
            part = dq[block * 32 : (block + 1) * 32]
            out[tile * (LAT_TILE // 32) + block, 64:80, :] = fold(part, 16).astype(BF)
    out[:, 0:32, :] = (dk_acc[...] * SCALE).astype(BF).reshape(32, 32, 128)
    out[:, 32:64, :] = dv_acc[...].astype(BF).reshape(32, 32, 128)


def tokens_of(ref, half, side, start):
    pieces = []
    for head in range(16):
        pieces.append(ref[2 * head + half, start : start + 32, side * 64 : (side + 1) * 64])
    return jnp.concatenate(pieces, axis=1)


def join_kernel(folded, out):
    for half in range(2):
        for side in range(2):
            at = half * 64 + side * 32
            out[at : at + 32, :] = tokens_of(folded, half, side, 0)


def key_kernel(own_t, other_t, own_dk, other_dk, out):
    part = dot(own_t[...], own_dk[...]) + dot(other_t[...], other_dk[...])
    out[...] = part.astype(BF).reshape(out.shape)


def post_kernel(dk, folded, w_query, w_key, w_value, prefix_grad, latent_grad, dv, dq):
    @pl.when(pl.program_id(0) == 0)
    def _():
        for half in range(2):
            for side in range(2):
                at = half * 64 + side * 32
                dv[at : at + 32, :] = tokens_of(folded, half, side, 32)
        for side in range(2):
            pieces = []
            for head in range(16):
                part = [folded[2 * head + half, 64:80, side * 64 : (side + 1) * 64].astype(F32) for half in range(2)]
                pieces.append(part[0] + part[1])
            dq[side * 16 : (side + 1) * 16, :] = jnp.concatenate(pieces, axis=1).astype(BF)

    prefix_grad[...] = (dot_nt(dk[...], w_key[...]) + dot_nt(dv[...], w_value[...])).astype(BF)
    latent_grad[...] = dot_nt(dq[...], w_query[...]).astype(BF)


def call(kernel, out_shape, flops=0, nbytes=0, limit=48, **kwargs):
    return pl.pallas_call(
        kernel,
        out_shape=out_shape,
        compiler_params=pltpu.CompilerParams(vmem_limit_bytes=limit << 20),
        cost_estimate=pl.CostEstimate(flops=flops, bytes_accessed=nbytes, transcendentals=0),
        **kwargs,
    )


def on_device(prefix, latents, saved, grad, visible, w_query, w_key, w_value):
    prefix, latents, saved, grad = prefix[0], latents[0], saved[0], grad[0]
    vis_row = visible
    vis_flat = visible[0]
    half = jnp.reshape(lax.axis_index("z") % 2, (1,)).astype(jnp.int32)
    core = lax.axis_index("core")
    vmem = pl.BlockSpec(memory_space=pltpu.VMEM)
    smem = pl.BlockSpec(memory_space=pltpu.SMEM)
    shape = jax.ShapeDtypeStruct

    whole = lambda rows: pl.BlockSpec((rows, 1024), lambda i: (0, 0))
    cols = lambda rows: pl.BlockSpec((rows, 256), lambda i: (0, i))
    at = lax.broadcasted_iota(jnp.int32, (1024, 1024), 0)
    c_at, y_at, x_at, z_at, k_at = at >> 9, (at >> 7) & 3, (at >> 5) & 3, (at >> 2) & 7, at & 3
    c_at = jnp.where(core == 0, c_at, 1 - c_at)
    wanted = (y_at * 8 + z_at) * 32 + x_at * 8 + c_at * 4 + k_at
    pick = (wanted == lax.broadcasted_iota(jnp.int32, (1024, 1024), 1)).astype(BF)
    prefix_t = dot_nt(pick, prefix).astype(BF)
    own_t = prefix_t[:512]
    other_t = lax.ppermute(prefix_t[512:], "core", [(0, 1), (1, 0)])

    data = call(
        pre_kernel,
        shape((32, 104, 128), BF),
        limit=60,
        flops=2 * 288 * 1024 * 1024,
        nbytes=8 << 20,
        grid=(4,),
        in_specs=[whole(128), whole(32), cols(32), cols(32), cols(1024), cols(1024), cols(1024)],
        out_specs=pl.BlockSpec((8, 104, 128), lambda i: (i, 0, 0)),
    )(prefix, latents, grad, saved, w_query, w_key, w_value)
    data = lax.all_to_all(data, ("y", "z"), 0, 0, tiled=True)

    stats = call(
        stats_kernel,
        shape((8, 1024), F32),
        flops=2 * 1024 * 2048 * 64,
        nbytes=1 << 19,
        in_specs=[smem, smem, vmem, vmem],
        out_specs=vmem,
        scratch_shapes=[pltpu.VMEM((1024, 128), BF)] * 2,
    )(vis_flat, half, vis_row, data)
    other = lax.ppermute(stats, "z", [(i, i ^ 1) for i in range(8)])
    back = call(
        grad_kernel,
        shape((32, 80, 128), BF),
        flops=10 * 1024 * 2048 * 64,
        nbytes=1 << 20,
        in_specs=[smem, smem] + [vmem] * 4,
        out_specs=vmem,
        scratch_shapes=[pltpu.VMEM((1024, 128), BF)] * 4
        + [
            pltpu.VMEM((32 // SRC_CHUNK, DH, SRC_CHUNK * 64), BF),
            pltpu.VMEM((1024, 128), F32),
            pltpu.VMEM((1024, 128), F32),
            pltpu.VMEM((1, 1024), F32),
        ],
    )(vis_flat, half, vis_row, data, stats, other)
    back = lax.all_to_all(back, ("y", "z"), 0, 0, tiled=True)

    dk = call(
        join_kernel,
        shape((128, 1024), BF),
        nbytes=1 << 19,
        in_specs=[vmem],
        out_specs=vmem,
    )(back)
    dk_other = lax.ppermute(dk, "core", [(0, 1), (1, 0)])
    part = call(
        key_kernel,
        shape((16, 32, 1024), BF),
        flops=2 * 512 * 256 * 1024,
        nbytes=2 << 20,
        in_specs=[vmem] * 4,
        out_specs=vmem,
    )(own_t, other_t, dk, dk_other)
    part = lax.all_to_all(part, ("y", "x"), 0, 0, tiled=True)
    part = jnp.sum(part.astype(F32), axis=0)
    part = lax.all_to_all(part.reshape(8, 4, 1024), "z", 0, 0, tiled=True)
    key_wgrad = jnp.sum(part, axis=0)

    rows = lambda n: pl.BlockSpec((256, 1024), lambda i: (i, 0))
    prefix_grad, latent_grad = call(
        post_kernel,
        (shape((128, 1024), BF), shape((32, 1024), BF)),
        limit=60,
        flops=2 * 288 * 1024 * 1024,
        nbytes=8 << 20,
        grid=(4,),
        in_specs=[whole(128), pl.BlockSpec((32, 80, 128), lambda i: (0, 0, 0))] + [rows(256)] * 3,
        out_specs=(cols(128), cols(32)),
        scratch_shapes=[pltpu.VMEM((128, 1024), BF), pltpu.VMEM((32, 1024), BF)],
    )(dk, back, w_query, w_key, w_value)
    return prefix_grad[None], latent_grad[None], key_wgrad


def solution(mesh):
    grid = Mesh(mesh.devices.reshape(4, 8, 4, 2), ("y", "z", "x", "core"))
    seq, dp = ("y", "z"), ("x", "core")
    return jax.shard_map(
        on_device,
        mesh=grid,
        in_specs=(
            P(dp, seq, None),
            P(dp, seq, None),
            P(dp, seq, None),
            P(dp, seq, None),
            P(dp, None),
            P(),
            P(),
            P(),
        ),
        out_specs=(P(dp, seq, None), P(dp, seq, None), P(seq + dp, None)),
        check_vma=False,
    )
```

```python
import functools
import math

import jax
import jax.numpy as jnp
from jax import lax
from jax.experimental import pallas as pl
from jax.experimental.pallas import tpu as pltpu
from jax.sharding import Mesh, PartitionSpec as P

BF = jnp.bfloat16
F32 = jnp.float32
DH = 64
NEG = -1e30
FLOOR = -1e29
SCALE = 1.0 / math.sqrt(DH)
C = SCALE * math.log2(math.e)
NT_DIMS = (((1,), (1,)), ((), ()))
LAT_TILE = 512
SRC_CHUNK = 16


def dot(a, b):
    return jnp.dot(a, b, preferred_element_type=F32)


def dot_nt(a, b):
    return lax.dot_general(a, b, NT_DIMS, preferred_element_type=F32)


def swap(x):
    return jnp.concatenate([x[..., 64:], x[..., :64]], axis=-1)


def fold(x, rows):
    return jnp.concatenate([x[:rows], x[rows:]], axis=1)


def pre_kernel(prefix, latents, grad, saved, w_query, w_key, w_value, out):
    keys = dot(prefix[...], w_key[...]).astype(BF)
    values = dot(prefix[...], w_value[...]).astype(BF)
    queries = dot(latents[...], w_query[...]).astype(BF)
    g = grad[...]
    product = g.astype(F32) * saved[...].astype(F32)
    product = jnp.concatenate([product, jnp.zeros((96, product.shape[1]), F32)], axis=0).T
    row = lax.broadcasted_iota(jnp.int32, (8, 128), 0)
    for head in range(8):
        cols = slice(head * DH, (head + 1) * DH)
        delta = jnp.sum(product[cols], axis=0, keepdims=True)
        high = delta.astype(BF).astype(F32)
        mid = (delta - high).astype(BF).astype(F32)
        low = delta - high - mid
        parts = jnp.where(row == 0, high, jnp.where(row == 1, mid, jnp.where(row == 2, low, 0.0)))
        q_fold = fold(queries[:, cols], 16)
        g_fold = fold(g[:, cols], 16)
        for half in range(2):
            toks = slice(half * 64, (half + 1) * 64)
            dest = 2 * head + half
            out[dest, 0:32, :] = fold(keys[toks, cols], 32)
            out[dest, 32:64, :] = fold(values[toks, cols], 32)
            out[dest, 64:80, :] = q_fold
            out[dest, 80:96, :] = g_fold
            out[dest, 96:104, :] = parts.astype(BF)


def unfold(folded, low_ref, high_ref):
    lane = lax.broadcasted_iota(jnp.int32, folded.shape, 2)
    other = swap(folded)
    zero = jnp.zeros_like(folded)
    left = lane < 64
    low = jnp.concatenate([jnp.where(left, folded, zero), jnp.where(left, other, zero)], axis=1)
    high = jnp.concatenate([jnp.where(left, zero, other), jnp.where(left, zero, folded)], axis=1)
    low_ref[...] = low.reshape(low_ref.shape)
    high_ref[...] = high.reshape(high_ref.shape)


SPAN = SRC_CHUNK * 128
ROWS = SRC_CHUNK * 32
CHUNKS = 32 // SRC_CHUNK


def hide(scores, bound):
    parts = scores.reshape(SRC_CHUNK, 32, LAT_TILE)
    row = lax.broadcasted_iota(jnp.int32, (1, 32, LAT_TILE), 1)
    first = lax.broadcasted_iota(jnp.int32, (SRC_CHUNK, 1, LAT_TILE), 0) * 128
    return jnp.where(row < bound[None] - first, parts, NEG).reshape(ROWS, LAT_TILE)


def all_chunks(step, carry):
    for chunk in range(CHUNKS):
        carry = step(chunk, carry)
    return carry


def stats_kernel(half_s, vis, data, out, q_low, q_high):
    half = half_s[0]
    unfold(data[:, 64:80, :], q_low, q_high)
    for tile in range(1024 // LAT_TILE):
        lanes = slice(tile * LAT_TILE, (tile + 1) * LAT_TILE)
        seen = vis[:, lanes] - half * 64
        ql = q_low[lanes, :]
        qh = q_high[lanes, :]

        def step(chunk, carry):
            top, total = carry
            k = data[slice(chunk * SRC_CHUNK, (chunk + 1) * SRC_CHUNK), 0:32, :].reshape(ROWS, 128)
            s_low = hide(dot_nt(k, ql), seen - chunk * SPAN)
            s_high = hide(dot_nt(k, qh), seen - 32 - chunk * SPAN)
            new = jnp.max(jnp.maximum(s_low, s_high), axis=0, keepdims=True)
            new = jnp.maximum(new, top)
            part = jnp.sum(jnp.exp2((s_low - new) * C) + jnp.exp2((s_high - new) * C), axis=0, keepdims=True)
            return new, total * jnp.exp2((top - new) * C) + part

        start = (jnp.full((1, LAT_TILE), FLOOR, F32), jnp.zeros((1, LAT_TILE), F32))
        top, total = all_chunks(step, start)
        out[0:1, lanes] = top
        out[1:2, lanes] = total
    out[2:8, :] = jnp.zeros((6, 1024), F32)


def grad_kernel(half_s, vis, data, own, other, out,
                q_low, q_high, g_low, g_high, k_t, dk_acc, dv_acc, delta_ref):
    half = half_s[0]
    unfold(data[:, 64:80, :], q_low, q_high)
    unfold(data[:, 80:96, :], g_low, g_high)
    for chunk in range(CHUNKS):
        k = data[chunk * SRC_CHUNK : (chunk + 1) * SRC_CHUNK, 0:32, :].reshape(ROWS, 128)
        turned = k.T
        k_t[chunk] = jnp.concatenate([turned[0:64], turned[64:128]], axis=1)
    dk_acc[...] = jnp.zeros_like(dk_acc)
    dv_acc[...] = jnp.zeros_like(dv_acc)
    lane = lax.broadcasted_iota(jnp.int32, (1, 128), 1)
    for block in range(8):
        joined = jnp.zeros((1, 128), F32)
        for place in range(4):
            parts = data[4 * block + place, 96:104, :].astype(F32)
            parts = jnp.sum(parts, axis=0, keepdims=True)
            if place:
                parts = pltpu.roll(parts, 32 * place, 1)
            joined = jnp.where((lane >> 5) == place, parts, joined)
        delta_ref[:, block * 128 : (block + 1) * 128] = joined
    top = jnp.maximum(own[0:1, :], other[0:1, :])
    total = own[1:2, :] * jnp.exp2((own[0:1, :] - top) * C) + other[1:2, :] * jnp.exp2((other[0:1, :] - top) * C)
    lse = top + jnp.log2(total) * (1.0 / C)
    for tile in range(1024 // LAT_TILE):
        lanes = slice(tile * LAT_TILE, (tile + 1) * LAT_TILE)
        seen = vis[:, lanes] - half * 64
        lse_t = lse[:, lanes]
        delta = delta_ref[:, lanes]
        ql, qh, gl, gh = q_low[lanes, :], q_high[lanes, :], g_low[lanes, :], g_high[lanes, :]

        def step(chunk, dq):
            srcs = slice(chunk * SRC_CHUNK, (chunk + 1) * SRC_CHUNK)
            k = data[srcs, 0:32, :].reshape(ROWS, 128)
            v = data[srcs, 32:64, :].reshape(ROWS, 128)
            s_low = hide(dot_nt(k, ql), seen - chunk * SPAN)
            s_high = hide(dot_nt(k, qh), seen - 32 - chunk * SPAN)
            p_low = jnp.exp2((s_low - lse_t) * C)
            p_high = jnp.exp2((s_high - lse_t) * C)
            ds_low = (p_low * (dot_nt(v, gl) - delta)).astype(BF)
            ds_high = (p_high * (dot_nt(v, gh) - delta)).astype(BF)
            place = slice(chunk * ROWS, (chunk + 1) * ROWS)
            dv_acc[place, :] += dot(p_low.astype(BF), gl) + dot(p_high.astype(BF), gh)
            dk_acc[place, :] += dot(ds_low, ql) + dot(ds_high, qh)
            return dq + dot(k_t[chunk], jnp.concatenate([ds_low, ds_high], axis=0))

        dq = all_chunks(step, jnp.zeros((DH, LAT_TILE), F32))
        dq = (dq * SCALE).T
        for block in range(LAT_TILE // 32):
            part = dq[block * 32 : (block + 1) * 32]
            out[tile * (LAT_TILE // 32) + block, 64:80, :] = fold(part, 16).astype(BF)
    out[:, 0:32, :] = (dk_acc[...] * SCALE).astype(BF).reshape(32, 32, 128)
    out[:, 32:64, :] = dv_acc[...].astype(BF).reshape(32, 32, 128)


def tokens_of(ref, half, side, start):
    pieces = []
    for head in range(16):
        pieces.append(ref[2 * head + half, start : start + 32, side * 64 : (side + 1) * 64])
    return jnp.concatenate(pieces, axis=1)


def join_kernel(folded, out):
    for half in range(2):
        for side in range(2):
            at = half * 64 + side * 32
            out[at : at + 32, :] = tokens_of(folded, half, side, 0)


def key_kernel(own_t, far_t, dk_0, dk_1, dk_2, dk_3, out):
    total = dot(own_t[0], dk_0[...]) + dot(own_t[1], dk_1[...])
    total += dot(far_t[0], dk_2[...]) + dot(far_t[1], dk_3[...])
    for block in range(64):
        out[block] = total[4 * block : 4 * block + 4].astype(BF)


def post_kernel(dk, folded, w_query, w_key, w_value, prefix_grad, latent_grad, dv, dq):
    @pl.when(pl.program_id(0) == 0)
    def _():
        for half in range(2):
            for side in range(2):
                at = half * 64 + side * 32
                dv[at : at + 32, :] = tokens_of(folded, half, side, 32)
        for side in range(2):
            pieces = []
            for head in range(16):
                part = [folded[2 * head + half, 64:80, side * 64 : (side + 1) * 64].astype(F32) for half in range(2)]
                pieces.append(part[0] + part[1])
            dq[side * 16 : (side + 1) * 16, :] = jnp.concatenate(pieces, axis=1).astype(BF)

    prefix_grad[...] = (dot_nt(dk[...], w_key[...]) + dot_nt(dv[...], w_value[...])).astype(BF)
    latent_grad[...] = dot_nt(dq[...], w_query[...]).astype(BF)


def call(kernel, out_shape, flops=0, nbytes=0, limit=48, **kwargs):
    return pl.pallas_call(
        kernel,
        out_shape=out_shape,
        compiler_params=pltpu.CompilerParams(vmem_limit_bytes=limit << 20),
        cost_estimate=pl.CostEstimate(flops=flops, bytes_accessed=nbytes, transcendentals=0),
        **kwargs,
    )


VMEM = pl.BlockSpec(memory_space=pltpu.VMEM)
SMEM = pl.BlockSpec(memory_space=pltpu.SMEM)
shape = jax.ShapeDtypeStruct


def whole(rows):
    return pl.BlockSpec((rows, 1024), lambda i: (0, 0))


def cols(rows):
    return pl.BlockSpec((rows, 256), lambda i: (0, i))


def wide(rows):
    return pl.BlockSpec((rows, 512), lambda i: (0, i))


def run_pre(prefix, latents, grad, saved, w_query, w_key, w_value):
    return call(
        pre_kernel,
        shape((32, 104, 128), BF),
        limit=60,
        flops=2 * 288 * 1024 * 1024,
        nbytes=8 << 20,
        grid=(2,),
        in_specs=[whole(128), whole(32), wide(32), wide(32), wide(1024), wide(1024), wide(1024)],
        out_specs=pl.BlockSpec((16, 104, 128), lambda i: (i, 0, 0)),
    )(prefix, latents, grad, saved, w_query, w_key, w_value)


def run_stats(half, vis_row, data):
    return call(
        stats_kernel,
        shape((8, 1024), F32),
        flops=2 * 1024 * 2048 * 64,
        nbytes=1 << 19,
        in_specs=[SMEM, VMEM, VMEM],
        out_specs=VMEM,
        scratch_shapes=[pltpu.VMEM((1024, 128), BF)] * 2,
    )(half, vis_row, data)


def run_grad(half, vis_row, data, stats, other):
    return call(
        grad_kernel,
        shape((32, 80, 128), BF),
        flops=10 * 1024 * 2048 * 64,
        nbytes=1 << 20,
        in_specs=[SMEM] + [VMEM] * 4,
        out_specs=VMEM,
        scratch_shapes=[pltpu.VMEM((1024, 128), BF)] * 4
        + [
            pltpu.VMEM((32 // SRC_CHUNK, DH, SRC_CHUNK * 64), BF),
            pltpu.VMEM((1024, 128), F32),
            pltpu.VMEM((1024, 128), F32),
            pltpu.VMEM((1, 1024), F32),
        ],
    )(half, vis_row, data, stats, other)


def run_join(back):
    return call(join_kernel, shape((128, 1024), BF), nbytes=1 << 19, in_specs=[VMEM], out_specs=VMEM)(back)


def run_key(own_t, far_t, *dks):
    return call(
        key_kernel,
        shape((64, 4, 1024), BF),
        flops=2 * 256 * 512 * 1024,
        nbytes=2 << 20,
        in_specs=[VMEM] * 6,
        out_specs=VMEM,
    )(own_t, far_t, *dks)


def run_post(dk, back, w_query, w_key, w_value):
    rows = pl.BlockSpec((256, 1024), lambda i: (i, 0))
    return call(
        post_kernel,
        (shape((128, 1024), BF), shape((32, 1024), BF)),
        limit=60,
        flops=2 * 288 * 1024 * 1024,
        nbytes=8 << 20,
        grid=(4,),
        in_specs=[whole(128), pl.BlockSpec((32, 80, 128), lambda i: (0, 0, 0))] + [rows] * 3,
        out_specs=(cols(128), cols(32)),
        scratch_shapes=[pltpu.VMEM((128, 1024), BF), pltpu.VMEM((32, 1024), BF)],
    )(dk, back, w_query, w_key, w_value)


def pick_rows(x_low, core):
    at = lax.broadcasted_iota(jnp.int32, (1024, 1024), 0)
    x_to, core_to = x_low ^ (at >> 9), core ^ ((at >> 8) & 1)
    wanted = ((at >> 2) & 31) * 32 + ((at >> 7) & 1) * 16 + x_to * 8 + core_to * 4 + (at & 3)
    return (wanted == lax.broadcasted_iota(jnp.int32, (1024, 1024), 1)).astype(BF)


def on_device(prefix, latents, saved, grad, visible, w_query, w_key, w_value):
    prefix, latents, saved, grad = prefix[0], latents[0], saved[0], grad[0]
    half = jnp.reshape(lax.axis_index("z") % 2, (1,)).astype(jnp.int32)
    over_core = lambda v: lax.ppermute(v, "core", [(0, 1), (1, 0)])
    over_x = lambda v: lax.ppermute(v, "x_low", [(0, 1), (1, 0)])

    data = run_pre(prefix, latents, grad, saved, w_query, w_key, w_value)
    data = lax.all_to_all(data, ("y", "z"), 0, 0, tiled=True)
    picked = pick_rows(lax.axis_index("x_low"), lax.axis_index("core"))
    turned = dot_nt(picked, prefix).astype(BF).reshape(4, 256, 128)
    gained = over_core(jnp.stack([turned[1], turned[3]]))
    own_t = jnp.stack([turned[0], gained[0]])
    far_t = over_x(jnp.stack([turned[2], gained[1]]))

    stats = run_stats(half, visible, data)
    stats, own_t, far_t = lax.optimization_barrier((stats, own_t, far_t))
    other = lax.ppermute(stats, "z", [(i, i ^ 1) for i in range(8)])
    back = run_grad(half, visible, data, stats, other)
    back = lax.all_to_all(back, ("y", "z"), 0, 0, tiled=True)

    dk = run_join(back)
    far_dk = over_x(dk)
    part = run_key(own_t, far_t, dk, over_core(dk), far_dk, over_core(far_dk))
    part = lax.all_to_all(part, ("x_high", "y", "z"), 0, 0, tiled=True)
    key_wgrad = jnp.sum(part.astype(F32), axis=0)
    prefix_grad, latent_grad = run_post(dk, back, w_query, w_key, w_value)
    return prefix_grad[None], latent_grad[None], key_wgrad


def solution(mesh):
    grid = Mesh(mesh.devices.reshape(4, 8, 2, 2, 2), ("y", "z", "x_high", "x_low", "core"))
    seq, dp = ("y", "z"), ("x_high", "x_low", "core")
    return jax.shard_map(
        on_device,
        mesh=grid,
        in_specs=(
            P(dp, seq, None),
            P(dp, seq, None),
            P(dp, seq, None),
            P(dp, seq, None),
            P(dp, None),
            P(),
            P(),
            P(),
        ),
        out_specs=(P(dp, seq, None), P(dp, seq, None), P(seq + dp, None)),
        check_vma=False,
    )
```

```python
import functools
import math

import jax
import jax.numpy as jnp
from jax import lax
from jax.experimental import pallas as pl
from jax.experimental.pallas import tpu as pltpu
from jax.sharding import Mesh, PartitionSpec as P

BF = jnp.bfloat16
F32 = jnp.float32
DH = 64
NEG = -1e30
FLOOR = -1e29
SCALE = 1.0 / math.sqrt(DH)
C = SCALE * math.log2(math.e)
NT_DIMS = (((1,), (1,)), ((), ()))
LAT_TILE = 512
SRC_CHUNK = 16


def dot(a, b):
    return jnp.dot(a, b, preferred_element_type=F32)


def dot_nt(a, b):
    return lax.dot_general(a, b, NT_DIMS, preferred_element_type=F32)


def swap(x):
    return jnp.concatenate([x[..., 64:], x[..., :64]], axis=-1)


def fold(x, rows):
    return jnp.concatenate([x[:rows], x[rows:]], axis=1)


def pre_kernel(prefix, latents, grad, saved, w_query, w_key, w_value, out):
    keys = dot(prefix[...], w_key[...]).astype(BF)
    values = dot(prefix[...], w_value[...]).astype(BF)
    queries = dot(latents[...], w_query[...]).astype(BF)
    g = grad[...]
    product = g.astype(F32) * saved[...].astype(F32)
    product = jnp.concatenate([product, jnp.zeros((96, product.shape[1]), F32)], axis=0).T
    row = lax.broadcasted_iota(jnp.int32, (8, 128), 0)
    for head in range(8):
        cols = slice(head * DH, (head + 1) * DH)
        delta = jnp.sum(product[cols], axis=0, keepdims=True)
        high = delta.astype(BF).astype(F32)
        mid = (delta - high).astype(BF).astype(F32)
        low = delta - high - mid
        parts = jnp.where(row == 0, high, jnp.where(row == 1, mid, jnp.where(row == 2, low, 0.0)))
        q_fold = fold(queries[:, cols], 16)
        g_fold = fold(g[:, cols], 16)
        for half in range(2):
            toks = slice(half * 64, (half + 1) * 64)
            dest = 2 * head + half
            out[dest, 0:32, :] = fold(keys[toks, cols], 32)
            out[dest, 32:64, :] = fold(values[toks, cols], 32)
            out[dest, 64:80, :] = q_fold
            out[dest, 80:96, :] = g_fold
            out[dest, 96:104, :] = parts.astype(BF)


def unfold(folded, low_ref, high_ref):
    lane = lax.broadcasted_iota(jnp.int32, folded.shape, 2)
    other = swap(folded)
    zero = jnp.zeros_like(folded)
    left = lane < 64
    low = jnp.concatenate([jnp.where(left, folded, zero), jnp.where(left, other, zero)], axis=1)
    high = jnp.concatenate([jnp.where(left, zero, other), jnp.where(left, zero, folded)], axis=1)
    low_ref[...] = low.reshape(low_ref.shape)
    high_ref[...] = high.reshape(high_ref.shape)


SPAN = SRC_CHUNK * 128
ROWS = SRC_CHUNK * 32
CHUNKS = 32 // SRC_CHUNK


def hide(scores, bound):
    parts = scores.reshape(SRC_CHUNK, 32, LAT_TILE)
    row = lax.broadcasted_iota(jnp.int32, (1, 32, LAT_TILE), 1)
    first = lax.broadcasted_iota(jnp.int32, (SRC_CHUNK, 1, LAT_TILE), 0) * 128
    return jnp.where(row < bound[None] - first, parts, NEG).reshape(ROWS, LAT_TILE)


def all_chunks(step, carry):
    for chunk in range(CHUNKS):
        carry = step(chunk, carry)
    return carry


def stats_kernel(half_s, vis, data, out, scores, q_low, q_high):
    half = half_s[0]
    unfold(data[:, 64:80, :], q_low, q_high)
    for tile in range(1024 // LAT_TILE):
        lanes = slice(tile * LAT_TILE, (tile + 1) * LAT_TILE)
        seen = vis[:, lanes] - half * 64
        ql = q_low[lanes, :]
        qh = q_high[lanes, :]

        def step(chunk, carry):
            top, total = carry
            k = data[slice(chunk * SRC_CHUNK, (chunk + 1) * SRC_CHUNK), 0:32, :].reshape(ROWS, 128)
            s_low = hide(dot_nt(k, ql), seen - chunk * SPAN)
            s_high = hide(dot_nt(k, qh), seen - 32 - chunk * SPAN)
            place = slice(chunk * ROWS, (chunk + 1) * ROWS)
            scores[0, place, lanes] = s_low
            scores[1, place, lanes] = s_high
            new = jnp.max(jnp.maximum(s_low, s_high), axis=0, keepdims=True)
            new = jnp.maximum(new, top)
            part = jnp.sum(jnp.exp2((s_low - new) * C) + jnp.exp2((s_high - new) * C), axis=0, keepdims=True)
            return new, total * jnp.exp2((top - new) * C) + part

        start = (jnp.full((1, LAT_TILE), FLOOR, F32), jnp.zeros((1, LAT_TILE), F32))
        top, total = all_chunks(step, start)
        out[0:1, lanes] = top
        out[1:2, lanes] = total
    out[2:8, :] = jnp.zeros((6, 1024), F32)


def dprobs_kernel(data, out, g_low, g_high, delta_ref):
    unfold(data[:, 80:96, :], g_low, g_high)
    lane = lax.broadcasted_iota(jnp.int32, (1, 128), 1)
    for block in range(8):
        joined = jnp.zeros((1, 128), F32)
        for place in range(4):
            parts = data[4 * block + place, 96:104, :].astype(F32)
            parts = jnp.sum(parts, axis=0, keepdims=True)
            if place:
                parts = pltpu.roll(parts, 32 * place, 1)
            joined = jnp.where((lane >> 5) == place, parts, joined)
        delta_ref[:, block * 128 : (block + 1) * 128] = joined
    for chunk in range(CHUNKS):
        place = slice(chunk * ROWS, (chunk + 1) * ROWS)
        v = data[chunk * SRC_CHUNK : (chunk + 1) * SRC_CHUNK, 32:64, :].reshape(ROWS, 128)
        for tile in range(1024 // LAT_TILE):
            lanes = slice(tile * LAT_TILE, (tile + 1) * LAT_TILE)
            out[0, place, lanes] = dot_nt(v, g_low[lanes, :]) - delta_ref[:, lanes]
            out[1, place, lanes] = dot_nt(v, g_high[lanes, :]) - delta_ref[:, lanes]


def grad_kernel(data, scores, dprobs, own, other, out, q_low, q_high, g_low, g_high, k_t, dk_acc, dv_acc):
    unfold(data[:, 64:80, :], q_low, q_high)
    unfold(data[:, 80:96, :], g_low, g_high)
    for chunk in range(CHUNKS):
        k = data[chunk * SRC_CHUNK : (chunk + 1) * SRC_CHUNK, 0:32, :].reshape(ROWS, 128)
        turned = k.T
        k_t[chunk] = jnp.concatenate([turned[0:64], turned[64:128]], axis=1)
    dk_acc[...] = jnp.zeros_like(dk_acc)
    dv_acc[...] = jnp.zeros_like(dv_acc)
    top = jnp.maximum(own[0:1, :], other[0:1, :])
    total = own[1:2, :] * jnp.exp2((own[0:1, :] - top) * C) + other[1:2, :] * jnp.exp2((other[0:1, :] - top) * C)
    lse = top + jnp.log2(total) * (1.0 / C)
    for tile in range(1024 // LAT_TILE):
        lanes = slice(tile * LAT_TILE, (tile + 1) * LAT_TILE)
        lse_t = lse[:, lanes]
        ql, qh, gl, gh = q_low[lanes, :], q_high[lanes, :], g_low[lanes, :], g_high[lanes, :]

        def step(chunk, dq):
            place = slice(chunk * ROWS, (chunk + 1) * ROWS)
            p_low = jnp.exp2((scores[0, place, lanes] - lse_t) * C)
            p_high = jnp.exp2((scores[1, place, lanes] - lse_t) * C)
            ds_low = (p_low * dprobs[0, place, lanes]).astype(BF)
            ds_high = (p_high * dprobs[1, place, lanes]).astype(BF)
            dv_acc[place, :] += dot(p_low.astype(BF), gl) + dot(p_high.astype(BF), gh)
            dk_acc[place, :] += dot(ds_low, ql) + dot(ds_high, qh)
            return dq + dot(k_t[chunk], jnp.concatenate([ds_low, ds_high], axis=0))

        dq = all_chunks(step, jnp.zeros((DH, LAT_TILE), F32))
        dq = (dq * SCALE).T
        for block in range(LAT_TILE // 32):
            part = dq[block * 32 : (block + 1) * 32]
            out[tile * (LAT_TILE // 32) + block, 64:80, :] = fold(part, 16).astype(BF)
    out[:, 0:32, :] = (dk_acc[...] * SCALE).astype(BF).reshape(32, 32, 128)
    out[:, 32:64, :] = dv_acc[...].astype(BF).reshape(32, 32, 128)


def tokens_of(ref, half, side, start):
    pieces = []
    for head in range(16):
        pieces.append(ref[2 * head + half, start : start + 32, side * 64 : (side + 1) * 64])
    return jnp.concatenate(pieces, axis=1)


def join_kernel(folded, out):
    for half in range(2):
        for side in range(2):
            at = half * 64 + side * 32
            out[at : at + 32, :] = tokens_of(folded, half, side, 0)


def key_kernel(turned, dk_0, dk_1, dk_2, dk_3, out):
    dks = jnp.concatenate([dk_0[...], dk_1[...], dk_2[...], dk_3[...]], axis=0)
    total = dot(turned[...], dks)
    for block in range(64):
        out[block] = total[4 * block : 4 * block + 4].astype(BF)


def post_kernel(dk, folded, w_query, w_key, w_value, prefix_grad, latent_grad, dv, dq):
    @pl.when(pl.program_id(0) == 0)
    def _():
        for half in range(2):
            for side in range(2):
                at = half * 64 + side * 32
                dv[at : at + 32, :] = tokens_of(folded, half, side, 32)
        for side in range(2):
            pieces = []
            for head in range(16):
                part = [folded[2 * head + half, 64:80, side * 64 : (side + 1) * 64].astype(F32) for half in range(2)]
                pieces.append(part[0] + part[1])
            dq[side * 16 : (side + 1) * 16, :] = jnp.concatenate(pieces, axis=1).astype(BF)

    prefix_grad[...] = (dot_nt(dk[...], w_key[...]) + dot_nt(dv[...], w_value[...])).astype(BF)
    latent_grad[...] = dot_nt(dq[...], w_query[...]).astype(BF)


def call(kernel, out_shape, flops=0, nbytes=0, limit=24, **kwargs):
    return pl.pallas_call(
        kernel,
        out_shape=out_shape,
        compiler_params=pltpu.CompilerParams(vmem_limit_bytes=limit << 20),
        cost_estimate=pl.CostEstimate(flops=flops, bytes_accessed=nbytes, transcendentals=0),
        **kwargs,
    )


VMEM = pl.BlockSpec(memory_space=pltpu.VMEM)
SMEM = pl.BlockSpec(memory_space=pltpu.SMEM)
shape = jax.ShapeDtypeStruct


def whole(rows):
    return pl.BlockSpec((rows, 1024), lambda i: (0, 0))


def cols(rows):
    return pl.BlockSpec((rows, 256), lambda i: (0, i))


def wide(rows):
    return pl.BlockSpec((rows, 512), lambda i: (0, i))


def run_pre(prefix, latents, grad, saved, w_query, w_key, w_value):
    return call(
        pre_kernel,
        shape((32, 104, 128), BF),
        limit=60,
        flops=2 * 288 * 1024 * 1024,
        nbytes=8 << 20,
        grid=(2,),
        in_specs=[whole(128), whole(32), wide(32), wide(32), wide(1024), wide(1024), wide(1024)],
        out_specs=pl.BlockSpec((16, 104, 128), lambda i: (i, 0, 0)),
    )(prefix, latents, grad, saved, w_query, w_key, w_value)


def run_stats(half, vis_row, data):
    return call(
        stats_kernel,
        (shape((8, 1024), F32), shape((2, 1024, 1024), F32)),
        flops=2 * 1024 * 2048 * 64,
        nbytes=1 << 19,
        in_specs=[SMEM, VMEM, VMEM],
        out_specs=(VMEM, VMEM),
        scratch_shapes=[pltpu.VMEM((1024, 128), BF)] * 2,
    )(half, vis_row, data)


def run_dprobs(data):
    return call(
        dprobs_kernel,
        shape((2, 1024, 1024), F32),
        flops=2 * 1024 * 2048 * 64,
        nbytes=1 << 19,
        in_specs=[VMEM],
        out_specs=VMEM,
        scratch_shapes=[pltpu.VMEM((1024, 128), BF)] * 2 + [pltpu.VMEM((1, 1024), F32)],
    )(data)


def run_grad(data, scores, dprobs, stats, other):
    return call(
        grad_kernel,
        shape((32, 80, 128), BF),
        flops=6 * 1024 * 2048 * 64,
        nbytes=1 << 20,
        in_specs=[VMEM] * 5,
        out_specs=VMEM,
        scratch_shapes=[pltpu.VMEM((1024, 128), BF)] * 4
        + [
            pltpu.VMEM((CHUNKS, DH, SRC_CHUNK * 64), BF),
            pltpu.VMEM((1024, 128), F32),
            pltpu.VMEM((1024, 128), F32),
        ],
    )(data, scores, dprobs, stats, other)


def run_join(back):
    return call(join_kernel, shape((128, 1024), BF), nbytes=1 << 19, in_specs=[VMEM], out_specs=VMEM)(back)


def run_key(turned, *dks):
    return call(
        key_kernel,
        shape((64, 4, 1024), BF),
        flops=2 * 256 * 512 * 1024,
        nbytes=2 << 20,
        in_specs=[VMEM] * 5,
        out_specs=VMEM,
    )(turned, *dks)


def run_post(dk, back, w_query, w_key, w_value):
    rows = pl.BlockSpec((256, 1024), lambda i: (i, 0))
    return call(
        post_kernel,
        (shape((128, 1024), BF), shape((32, 1024), BF)),
        limit=60,
        flops=2 * 288 * 1024 * 1024,
        nbytes=8 << 20,
        grid=(4,),
        in_specs=[whole(128), pl.BlockSpec((32, 80, 128), lambda i: (0, 0, 0))] + [rows] * 3,
        out_specs=(cols(128), cols(32)),
        scratch_shapes=[pltpu.VMEM((128, 1024), BF), pltpu.VMEM((32, 1024), BF)],
    )(dk, back, w_query, w_key, w_value)


def pick_rows(x_low, core):
    at = lax.broadcasted_iota(jnp.int32, (1024, 1024), 0)
    x_to, core_to = x_low ^ (at >> 9), core ^ ((at >> 8) & 1)
    wanted = ((at >> 2) & 31) * 32 + ((at >> 7) & 1) * 16 + x_to * 8 + core_to * 4 + (at & 3)
    return (wanted == lax.broadcasted_iota(jnp.int32, (1024, 1024), 1)).astype(BF)


def on_device(prefix, latents, saved, grad, visible, w_query, w_key, w_value):
    prefix, latents, saved, grad = prefix[0], latents[0], saved[0], grad[0]
    half = jnp.reshape(lax.axis_index("z") % 2, (1,)).astype(jnp.int32)
    over_core = lambda v: lax.ppermute(v, "core", [(0, 1), (1, 0)])
    over_x = lambda v: lax.ppermute(v, "x_low", [(0, 1), (1, 0)])

    data = run_pre(prefix, latents, grad, saved, w_query, w_key, w_value)
    data = lax.all_to_all(data, ("y", "z"), 0, 0, tiled=True)
    picked = pick_rows(lax.axis_index("x_low"), lax.axis_index("core"))
    turned = dot_nt(picked, prefix).astype(BF).reshape(4, 256, 128)
    gained = over_core(jnp.stack([turned[1], turned[3]]))
    far_t = over_x(jnp.stack([turned[2], gained[1]]))
    turned = jnp.concatenate([turned[0], gained[0], far_t[0], far_t[1]], axis=1)

    stats, scores = run_stats(half, visible, data)
    stats, turned = lax.optimization_barrier((stats, turned))
    other = lax.ppermute(stats, "z", [(i, i ^ 1) for i in range(8)])
    dprobs = run_dprobs(data)
    back = run_grad(data, scores, dprobs, stats, other)
    back = lax.all_to_all(back, ("y", "z"), 0, 0, tiled=True)

    dk = run_join(back)
    far_dk = over_x(dk)
    part = run_key(turned, dk, over_core(dk), far_dk, over_core(far_dk))
    part = lax.all_to_all(part, ("x_high", "y", "z"), 0, 0, tiled=True)
    key_wgrad = jnp.sum(part.astype(F32), axis=0)
    prefix_grad, latent_grad = run_post(dk, back, w_query, w_key, w_value)
    return prefix_grad[None], latent_grad[None], key_wgrad


def solution(mesh):
    grid = Mesh(mesh.devices.reshape(4, 8, 2, 2, 2), ("y", "z", "x_high", "x_low", "core"))
    seq, dp = ("y", "z"), ("x_high", "x_low", "core")
    return jax.shard_map(
        on_device,
        mesh=grid,
        in_specs=(
            P(dp, seq, None),
            P(dp, seq, None),
            P(dp, seq, None),
            P(dp, seq, None),
            P(dp, None),
            P(),
            P(),
            P(),
        ),
        out_specs=(P(dp, seq, None), P(dp, seq, None), P(seq + dp, None)),
        check_vma=False,
    )
```

```python
import functools
import math

import jax
import jax.numpy as jnp
from jax import lax
from jax.experimental import pallas as pl
from jax.experimental.pallas import tpu as pltpu
from jax.sharding import Mesh, PartitionSpec as P

BF = jnp.bfloat16
F32 = jnp.float32
DH = 64
NEG = -1e30
FLOOR = -1e29
SCALE = 1.0 / math.sqrt(DH)
C = SCALE * math.log2(math.e)
NT_DIMS = (((1,), (1,)), ((), ()))
LAT_TILE = 512
SRC_CHUNK = 16


def dot(a, b):
    return jnp.dot(a, b, preferred_element_type=F32)


def dot_nt(a, b):
    return lax.dot_general(a, b, NT_DIMS, preferred_element_type=F32)


def swap(x):
    return jnp.concatenate([x[..., 64:], x[..., :64]], axis=-1)


def fold(x, rows):
    return jnp.concatenate([x[:rows], x[rows:]], axis=1)


def pre_kernel(prefix, latents, grad, saved, w_query, w_key, w_value, out):
    keys = dot(prefix[...], w_key[...]).astype(BF)
    values = dot(prefix[...], w_value[...]).astype(BF)
    queries = dot(latents[...], w_query[...]).astype(BF)
    g = grad[...]
    product = g.astype(F32) * saved[...].astype(F32)
    product = jnp.concatenate([product, jnp.zeros((96, product.shape[1]), F32)], axis=0).T
    row = lax.broadcasted_iota(jnp.int32, (8, 128), 0)
    for head in range(8):
        cols = slice(head * DH, (head + 1) * DH)
        delta = jnp.sum(product[cols], axis=0, keepdims=True)
        high = delta.astype(BF).astype(F32)
        mid = (delta - high).astype(BF).astype(F32)
        low = delta - high - mid
        parts = jnp.where(row == 0, high, jnp.where(row == 1, mid, jnp.where(row == 2, low, 0.0)))
        q_fold = fold(queries[:, cols], 16)
        g_fold = fold(g[:, cols], 16)
        for half in range(2):
            toks = slice(half * 64, (half + 1) * 64)
            dest = 2 * head + half
            out[dest, 0:32, :] = fold(keys[toks, cols], 32)
            out[dest, 32:64, :] = fold(values[toks, cols], 32)
            out[dest, 64:80, :] = q_fold
            out[dest, 80:96, :] = g_fold
            out[dest, 96:104, :] = parts.astype(BF)


def unfold(folded, low_ref, high_ref):
    lane = lax.broadcasted_iota(jnp.int32, folded.shape, 2)
    other = swap(folded)
    zero = jnp.zeros_like(folded)
    left = lane < 64
    low = jnp.concatenate([jnp.where(left, folded, zero), jnp.where(left, other, zero)], axis=1)
    high = jnp.concatenate([jnp.where(left, zero, other), jnp.where(left, zero, folded)], axis=1)
    low_ref[...] = low.reshape(low_ref.shape)
    high_ref[...] = high.reshape(high_ref.shape)


SPAN = SRC_CHUNK * 128
ROWS = SRC_CHUNK * 32
CHUNKS = 32 // SRC_CHUNK


def hide(scores, bound):
    parts = scores.reshape(SRC_CHUNK, 32, LAT_TILE)
    row = lax.broadcasted_iota(jnp.int32, (1, 32, LAT_TILE), 1)
    first = lax.broadcasted_iota(jnp.int32, (SRC_CHUNK, 1, LAT_TILE), 0) * 128
    return jnp.where(row < bound[None] - first, parts, NEG).reshape(ROWS, LAT_TILE)


def all_chunks(step, carry):
    for chunk in range(CHUNKS):
        carry = step(chunk, carry)
    return carry


def stats_kernel(half_s, vis, data, out, scores, q_low, q_high):
    half = half_s[0]
    unfold(data[:, 64:80, :], q_low, q_high)
    for tile in range(1024 // LAT_TILE):
        lanes = slice(tile * LAT_TILE, (tile + 1) * LAT_TILE)
        seen = vis[:, lanes] - half * 64
        ql = q_low[lanes, :]
        qh = q_high[lanes, :]

        def step(chunk, carry):
            top, total = carry
            k = data[slice(chunk * SRC_CHUNK, (chunk + 1) * SRC_CHUNK), 0:32, :].reshape(ROWS, 128)
            s_low = hide(dot_nt(k, ql), seen - chunk * SPAN)
            s_high = hide(dot_nt(k, qh), seen - 32 - chunk * SPAN)
            place = slice(chunk * ROWS, (chunk + 1) * ROWS)
            scores[0, place, lanes] = s_low
            scores[1, place, lanes] = s_high
            new = jnp.max(jnp.maximum(s_low, s_high), axis=0, keepdims=True)
            new = jnp.maximum(new, top)
            part = jnp.sum(jnp.exp2((s_low - new) * C) + jnp.exp2((s_high - new) * C), axis=0, keepdims=True)
            return new, total * jnp.exp2((top - new) * C) + part

        start = (jnp.full((1, LAT_TILE), FLOOR, F32), jnp.zeros((1, LAT_TILE), F32))
        top, total = all_chunks(step, start)
        out[0:1, lanes] = top
        out[1:2, lanes] = total
    out[2:8, :] = jnp.zeros((6, 1024), F32)


def dprobs_kernel(data, out, g_low, g_high, delta_ref):
    unfold(data[:, 80:96, :], g_low, g_high)
    lane = lax.broadcasted_iota(jnp.int32, (1, 128), 1)
    for block in range(8):
        joined = jnp.zeros((1, 128), F32)
        for place in range(4):
            parts = data[4 * block + place, 96:104, :].astype(F32)
            parts = jnp.sum(parts, axis=0, keepdims=True)
            if place:
                parts = pltpu.roll(parts, 32 * place, 1)
            joined = jnp.where((lane >> 5) == place, parts, joined)
        delta_ref[:, block * 128 : (block + 1) * 128] = joined
    for chunk in range(CHUNKS):
        place = slice(chunk * ROWS, (chunk + 1) * ROWS)
        v = data[chunk * SRC_CHUNK : (chunk + 1) * SRC_CHUNK, 32:64, :].reshape(ROWS, 128)
        for tile in range(1024 // LAT_TILE):
            lanes = slice(tile * LAT_TILE, (tile + 1) * LAT_TILE)
            out[0, place, lanes] = dot_nt(v, g_low[lanes, :]) - delta_ref[:, lanes]
            out[1, place, lanes] = dot_nt(v, g_high[lanes, :]) - delta_ref[:, lanes]


def grad_kernel(data, scores, dprobs, own, other, out, q_low, q_high, g_low, g_high, k_t, dk_acc, dv_acc):
    unfold(data[:, 64:80, :], q_low, q_high)
    unfold(data[:, 80:96, :], g_low, g_high)
    for chunk in range(CHUNKS):
        k = data[chunk * SRC_CHUNK : (chunk + 1) * SRC_CHUNK, 0:32, :].reshape(ROWS, 128)
        turned = k.T
        k_t[chunk] = jnp.concatenate([turned[0:64], turned[64:128]], axis=1)
    dk_acc[...] = jnp.zeros_like(dk_acc)
    dv_acc[...] = jnp.zeros_like(dv_acc)
    top = jnp.maximum(own[0:1, :], other[0:1, :])
    total = own[1:2, :] * jnp.exp2((own[0:1, :] - top) * C) + other[1:2, :] * jnp.exp2((other[0:1, :] - top) * C)
    lse = top + jnp.log2(total) * (1.0 / C)
    for tile in range(1024 // LAT_TILE):
        lanes = slice(tile * LAT_TILE, (tile + 1) * LAT_TILE)
        lse_t = lse[:, lanes]
        ql, qh, gl, gh = q_low[lanes, :], q_high[lanes, :], g_low[lanes, :], g_high[lanes, :]

        def step(chunk, dq):
            place = slice(chunk * ROWS, (chunk + 1) * ROWS)
            p_low = jnp.exp2((scores[0, place, lanes] - lse_t) * C)
            p_high = jnp.exp2((scores[1, place, lanes] - lse_t) * C)
            ds_low = (p_low * dprobs[0, place, lanes]).astype(BF)
            ds_high = (p_high * dprobs[1, place, lanes]).astype(BF)
            dv_acc[place, :] += dot(p_low.astype(BF), gl) + dot(p_high.astype(BF), gh)
            dk_acc[place, :] += dot(ds_low, ql) + dot(ds_high, qh)
            return dq + dot(k_t[chunk], jnp.concatenate([ds_low, ds_high], axis=0))

        dq = all_chunks(step, jnp.zeros((DH, LAT_TILE), F32))
        dq = (dq * SCALE).T
        for block in range(LAT_TILE // 32):
            part = dq[block * 32 : (block + 1) * 32]
            out[tile * (LAT_TILE // 32) + block, 64:80, :] = fold(part, 16).astype(BF)
    out[:, 0:32, :] = (dk_acc[...] * SCALE).astype(BF).reshape(32, 32, 128)
    out[:, 32:64, :] = dv_acc[...].astype(BF).reshape(32, 32, 128)


def tokens_of(ref, half, side, start):
    pieces = []
    for head in range(16):
        pieces.append(ref[2 * head + half, start : start + 32, side * 64 : (side + 1) * 64])
    return jnp.concatenate(pieces, axis=1)


def join_kernel(folded, out):
    for half in range(2):
        for side in range(2):
            at = half * 64 + side * 32
            out[at : at + 32, :] = tokens_of(folded, half, side, 0)


def key_kernel(turned, dk_0, dk_1, dk_2, dk_3, out):
    dks = jnp.concatenate([dk_0[...], dk_1[...], dk_2[...], dk_3[...]], axis=0)
    total = dot(turned[...], dks)
    for block in range(64):
        out[block] = total[4 * block : 4 * block + 4].astype(BF)


def post_kernel(dk, folded, w_query, w_key, w_value, prefix_grad, latent_grad, dv, dq):
    @pl.when(pl.program_id(0) == 0)
    def _():
        for half in range(2):
            for side in range(2):
                at = half * 64 + side * 32
                dv[at : at + 32, :] = tokens_of(folded, half, side, 32)
        for side in range(2):
            pieces = []
            for head in range(16):
                part = [folded[2 * head + half, 64:80, side * 64 : (side + 1) * 64].astype(F32) for half in range(2)]
                pieces.append(part[0] + part[1])
            dq[side * 16 : (side + 1) * 16, :] = jnp.concatenate(pieces, axis=1).astype(BF)

    prefix_grad[...] = (dot_nt(dk[...], w_key[...]) + dot_nt(dv[...], w_value[...])).astype(BF)
    latent_grad[...] = dot_nt(dq[...], w_query[...]).astype(BF)


def call(kernel, out_shape, flops=0, nbytes=0, limit=24, **kwargs):
    return pl.pallas_call(
        kernel,
        out_shape=out_shape,
        compiler_params=pltpu.CompilerParams(vmem_limit_bytes=limit << 20),
        cost_estimate=pl.CostEstimate(flops=flops, bytes_accessed=nbytes, transcendentals=0),
        **kwargs,
    )


VMEM = pl.BlockSpec(memory_space=pltpu.VMEM)
SMEM = pl.BlockSpec(memory_space=pltpu.SMEM)
shape = jax.ShapeDtypeStruct


def whole(rows):
    return pl.BlockSpec((rows, 1024), lambda i: (0, 0))


def cols(rows):
    return pl.BlockSpec((rows, 256), lambda i: (0, i))


def wide(rows):
    return pl.BlockSpec((rows, 512), lambda i: (0, i))


def run_pre(prefix, latents, grad, saved, w_query, w_key, w_value):
    return call(
        pre_kernel,
        shape((32, 104, 128), BF),
        limit=60,
        flops=2 * 288 * 1024 * 1024,
        nbytes=8 << 20,
        grid=(2,),
        in_specs=[whole(128), whole(32), wide(32), wide(32), wide(1024), wide(1024), wide(1024)],
        out_specs=pl.BlockSpec((16, 104, 128), lambda i: (i, 0, 0)),
    )(prefix, latents, grad, saved, w_query, w_key, w_value)


def run_stats(half, vis_row, data):
    return call(
        stats_kernel,
        (shape((8, 1024), F32), shape((2, 1024, 1024), F32)),
        flops=2 * 1024 * 2048 * 64,
        nbytes=1 << 19,
        in_specs=[SMEM, VMEM, VMEM],
        out_specs=(VMEM, VMEM),
        scratch_shapes=[pltpu.VMEM((1024, 128), BF)] * 2,
    )(half, vis_row, data)


def run_dprobs(data):
    return call(
        dprobs_kernel,
        shape((2, 1024, 1024), F32),
        flops=2 * 1024 * 2048 * 64,
        nbytes=1 << 19,
        in_specs=[VMEM],
        out_specs=VMEM,
        scratch_shapes=[pltpu.VMEM((1024, 128), BF)] * 2 + [pltpu.VMEM((1, 1024), F32)],
    )(data)


def run_grad(data, scores, dprobs, stats, other):
    return call(
        grad_kernel,
        shape((32, 80, 128), BF),
        flops=6 * 1024 * 2048 * 64,
        nbytes=1 << 20,
        in_specs=[VMEM] * 5,
        out_specs=VMEM,
        scratch_shapes=[pltpu.VMEM((1024, 128), BF)] * 4
        + [
            pltpu.VMEM((CHUNKS, DH, SRC_CHUNK * 64), BF),
            pltpu.VMEM((1024, 128), F32),
            pltpu.VMEM((1024, 128), F32),
        ],
    )(data, scores, dprobs, stats, other)


def run_join(back):
    return call(join_kernel, shape((128, 1024), BF), nbytes=1 << 19, in_specs=[VMEM], out_specs=VMEM)(back)


def run_key(turned, *dks):
    return call(
        key_kernel,
        shape((64, 4, 1024), BF),
        flops=2 * 256 * 512 * 1024,
        nbytes=2 << 20,
        in_specs=[VMEM] * 5,
        out_specs=VMEM,
    )(turned, *dks)


def run_post(dk, back, w_query, w_key, w_value):
    rows = pl.BlockSpec((256, 1024), lambda i: (i, 0))
    return call(
        post_kernel,
        (shape((128, 1024), BF), shape((32, 1024), BF)),
        limit=60,
        flops=2 * 288 * 1024 * 1024,
        nbytes=8 << 20,
        grid=(4,),
        in_specs=[whole(128), pl.BlockSpec((32, 80, 128), lambda i: (0, 0, 0))] + [rows] * 3,
        out_specs=(cols(128), cols(32)),
        scratch_shapes=[pltpu.VMEM((128, 1024), BF), pltpu.VMEM((32, 1024), BF)],
    )(dk, back, w_query, w_key, w_value)


def pick_rows(x_low, core):
    at = lax.broadcasted_iota(jnp.int32, (1024, 1024), 0)
    x_to, core_to = x_low ^ (at >> 9), core ^ ((at >> 8) & 1)
    wanted = ((at >> 3) & 31) * 32 + ((at >> 2) & 1) * 16 + x_to * 8 + core_to * 4 + (at & 3)
    return (wanted == lax.broadcasted_iota(jnp.int32, (1024, 1024), 1)).astype(BF)


def on_device(prefix, latents, saved, grad, visible, w_query, w_key, w_value):
    prefix, latents, saved, grad = prefix[0], latents[0], saved[0], grad[0]
    half = jnp.reshape(lax.axis_index("z") % 2, (1,)).astype(jnp.int32)
    over_core = lambda v: lax.ppermute(v, "core", [(0, 1), (1, 0)])
    over_x = lambda v: lax.ppermute(v, "x_low", [(0, 1), (1, 0)])

    data = run_pre(prefix, latents, grad, saved, w_query, w_key, w_value)
    data = lax.all_to_all(data, ("y", "z"), 0, 0, tiled=True)
    picked = pick_rows(lax.axis_index("x_low"), lax.axis_index("core"))
    turned = dot_nt(picked, prefix).astype(BF).reshape(4, 256, 128)
    gained = over_core(jnp.stack([turned[1], turned[3]]))
    far_t = over_x(jnp.stack([turned[2], gained[1]]))
    turned = jnp.concatenate([turned[0], gained[0], far_t[0], far_t[1]], axis=1)

    stats, scores = run_stats(half, visible, data)
    stats, turned = lax.optimization_barrier((stats, turned))
    other = lax.ppermute(stats, "z", [(i, i ^ 1) for i in range(8)])
    dprobs = run_dprobs(data)
    back = run_grad(data, scores, dprobs, stats, other)
    back = lax.all_to_all(back, ("y", "z"), 0, 0, tiled=True)

    dk = run_join(back)
    far_dk = over_x(dk)
    part = run_key(turned, dk, over_core(dk), far_dk, over_core(far_dk))
    part = lax.all_to_all(part, ("y", "z", "x_high"), 0, 0, tiled=True)
    key_wgrad = jnp.sum(part.astype(F32), axis=0)
    prefix_grad, latent_grad = run_post(dk, back, w_query, w_key, w_value)
    return prefix_grad[None], latent_grad[None], key_wgrad


def solution(mesh):
    grid = Mesh(mesh.devices.reshape(4, 8, 2, 2, 2), ("y", "z", "x_high", "x_low", "core"))
    seq, dp = ("y", "z"), ("x_high", "x_low", "core")
    return jax.shard_map(
        on_device,
        mesh=grid,
        in_specs=(
            P(dp, seq, None),
            P(dp, seq, None),
            P(dp, seq, None),
            P(dp, seq, None),
            P(dp, None),
            P(),
            P(),
            P(),
        ),
        out_specs=(P(dp, seq, None), P(dp, seq, None), P(seq + dp, None)),
        check_vma=False,
    )
```

```python
import functools
import math

import jax
import jax.numpy as jnp
from jax import lax
from jax.experimental import pallas as pl
from jax.experimental.pallas import tpu as pltpu
from jax.sharding import Mesh, PartitionSpec as P

BF = jnp.bfloat16
F32 = jnp.float32
DH = 64
NEG = -1e30
FLOOR = -1e29
SCALE = 1.0 / math.sqrt(DH)
C = SCALE * math.log2(math.e)
NT_DIMS = (((1,), (1,)), ((), ()))
LAT_TILE = 512
SRC_CHUNK = 16


def dot(a, b):
    return jnp.dot(a, b, preferred_element_type=F32)


def dot_nt(a, b):
    return lax.dot_general(a, b, NT_DIMS, preferred_element_type=F32)


def swap(x):
    return jnp.concatenate([x[..., 64:], x[..., :64]], axis=-1)


def fold(x, rows):
    return jnp.concatenate([x[:rows], x[rows:]], axis=1)


def pre_kernel(prefix, latents, grad, saved, w_query, w_key, w_value, out):
    keys = dot(prefix[...], w_key[...]).astype(BF)
    values = dot(prefix[...], w_value[...]).astype(BF)
    queries = dot(latents[...], w_query[...]).astype(BF)
    g = grad[...]
    product = g.astype(F32) * saved[...].astype(F32)
    product = jnp.concatenate([product, jnp.zeros((96, product.shape[1]), F32)], axis=0).T
    row = lax.broadcasted_iota(jnp.int32, (8, 128), 0)
    for head in range(8):
        cols = slice(head * DH, (head + 1) * DH)
        delta = jnp.sum(product[cols], axis=0, keepdims=True)
        high = delta.astype(BF).astype(F32)
        mid = (delta - high).astype(BF).astype(F32)
        low = delta - high - mid
        parts = jnp.where(row == 0, high, jnp.where(row == 1, mid, jnp.where(row == 2, low, 0.0)))
        q_fold = fold(queries[:, cols], 16)
        g_fold = fold(g[:, cols], 16)
        for half in range(2):
            toks = slice(half * 64, (half + 1) * 64)
            dest = 2 * head + half
            out[dest, 0:32, :] = fold(keys[toks, cols], 32)
            out[dest, 32:64, :] = fold(values[toks, cols], 32)
            out[dest, 64:80, :] = q_fold
            out[dest, 80:96, :] = g_fold
            out[dest, 96:104, :] = parts.astype(BF)


def unfold(folded, low_ref, high_ref):
    lane = lax.broadcasted_iota(jnp.int32, folded.shape, 2)
    other = swap(folded)
    zero = jnp.zeros_like(folded)
    left = lane < 64
    low = jnp.concatenate([jnp.where(left, folded, zero), jnp.where(left, other, zero)], axis=1)
    high = jnp.concatenate([jnp.where(left, zero, other), jnp.where(left, zero, folded)], axis=1)
    low_ref[...] = low.reshape(low_ref.shape)
    high_ref[...] = high.reshape(high_ref.shape)


SPAN = SRC_CHUNK * 128
ROWS = SRC_CHUNK * 32
CHUNKS = 32 // SRC_CHUNK


def hide(scores, bound):
    parts = scores.reshape(SRC_CHUNK, 32, LAT_TILE)
    row = lax.broadcasted_iota(jnp.int32, (1, 32, LAT_TILE), 1)
    first = lax.broadcasted_iota(jnp.int32, (SRC_CHUNK, 1, LAT_TILE), 0) * 128
    return jnp.where(row < bound[None] - first, parts, NEG).reshape(ROWS, LAT_TILE)


def all_chunks(step, carry):
    for chunk in range(CHUNKS):
        carry = step(chunk, carry)
    return carry


def stats_kernel(half_s, vis, data, out, scores, q_low, q_high):
    half = half_s[0]
    unfold(data[:, 64:80, :], q_low, q_high)
    for tile in range(1024 // LAT_TILE):
        lanes = slice(tile * LAT_TILE, (tile + 1) * LAT_TILE)
        seen = vis[:, lanes] - half * 64
        ql = q_low[lanes, :]
        qh = q_high[lanes, :]

        def step(chunk, carry):
            top, total = carry
            k = data[slice(chunk * SRC_CHUNK, (chunk + 1) * SRC_CHUNK), 0:32, :].reshape(ROWS, 128)
            s_low = hide(dot_nt(k, ql), seen - chunk * SPAN)
            s_high = hide(dot_nt(k, qh), seen - 32 - chunk * SPAN)
            place = slice(chunk * ROWS, (chunk + 1) * ROWS)
            scores[0, place, lanes] = s_low
            scores[1, place, lanes] = s_high
            new = jnp.max(jnp.maximum(s_low, s_high), axis=0, keepdims=True)
            new = jnp.maximum(new, top)
            part = jnp.sum(jnp.exp2((s_low - new) * C) + jnp.exp2((s_high - new) * C), axis=0, keepdims=True)
            return new, total * jnp.exp2((top - new) * C) + part

        start = (jnp.full((1, LAT_TILE), FLOOR, F32), jnp.zeros((1, LAT_TILE), F32))
        top, total = all_chunks(step, start)
        out[0:1, lanes] = top
        out[1:2, lanes] = total
    out[2:8, :] = jnp.zeros((6, 1024), F32)


def dprobs_kernel(data, out, g_low, g_high, delta_ref):
    unfold(data[:, 80:96, :], g_low, g_high)
    lane = lax.broadcasted_iota(jnp.int32, (1, 128), 1)
    for block in range(8):
        joined = jnp.zeros((1, 128), F32)
        for place in range(4):
            parts = data[4 * block + place, 96:104, :].astype(F32)
            parts = jnp.sum(parts, axis=0, keepdims=True)
            if place:
                parts = pltpu.roll(parts, 32 * place, 1)
            joined = jnp.where((lane >> 5) == place, parts, joined)
        delta_ref[:, block * 128 : (block + 1) * 128] = joined
    for chunk in range(CHUNKS):
        place = slice(chunk * ROWS, (chunk + 1) * ROWS)
        v = data[chunk * SRC_CHUNK : (chunk + 1) * SRC_CHUNK, 32:64, :].reshape(ROWS, 128)
        for tile in range(1024 // LAT_TILE):
            lanes = slice(tile * LAT_TILE, (tile + 1) * LAT_TILE)
            out[0, place, lanes] = dot_nt(v, g_low[lanes, :]) - delta_ref[:, lanes]
            out[1, place, lanes] = dot_nt(v, g_high[lanes, :]) - delta_ref[:, lanes]


def grad_kernel(data, scores, dprobs, own, other, out, q_low, q_high, g_low, g_high, k_t, dk_acc, dv_acc):
    unfold(data[:, 64:80, :], q_low, q_high)
    unfold(data[:, 80:96, :], g_low, g_high)
    for chunk in range(CHUNKS):
        k = data[chunk * SRC_CHUNK : (chunk + 1) * SRC_CHUNK, 0:32, :].reshape(ROWS, 128)
        turned = k.T
        k_t[chunk] = jnp.concatenate([turned[0:64], turned[64:128]], axis=1)
    dk_acc[...] = jnp.zeros_like(dk_acc)
    dv_acc[...] = jnp.zeros_like(dv_acc)
    top = jnp.maximum(own[0:1, :], other[0:1, :])
    total = own[1:2, :] * jnp.exp2((own[0:1, :] - top) * C) + other[1:2, :] * jnp.exp2((other[0:1, :] - top) * C)
    lse = top + jnp.log2(total) * (1.0 / C)
    for tile in range(1024 // LAT_TILE):
        lanes = slice(tile * LAT_TILE, (tile + 1) * LAT_TILE)
        lse_t = lse[:, lanes]
        ql, qh, gl, gh = q_low[lanes, :], q_high[lanes, :], g_low[lanes, :], g_high[lanes, :]

        def step(chunk, dq):
            place = slice(chunk * ROWS, (chunk + 1) * ROWS)
            p_low = jnp.exp2((scores[0, place, lanes] - lse_t) * C)
            p_high = jnp.exp2((scores[1, place, lanes] - lse_t) * C)
            ds_low = (p_low * dprobs[0, place, lanes]).astype(BF)
            ds_high = (p_high * dprobs[1, place, lanes]).astype(BF)
            dv_acc[place, :] += dot(p_low.astype(BF), gl) + dot(p_high.astype(BF), gh)
            dk_acc[place, :] += dot(ds_low, ql) + dot(ds_high, qh)
            return dq + dot(k_t[chunk], jnp.concatenate([ds_low, ds_high], axis=0))

        dq = all_chunks(step, jnp.zeros((DH, LAT_TILE), F32))
        dq = (dq * SCALE).T
        for block in range(LAT_TILE // 32):
            part = dq[block * 32 : (block + 1) * 32]
            out[tile * (LAT_TILE // 32) + block, 64:80, :] = fold(part, 16).astype(BF)
    out[:, 0:32, :] = (dk_acc[...] * SCALE).astype(BF).reshape(32, 32, 128)
    out[:, 32:64, :] = dv_acc[...].astype(BF).reshape(32, 32, 128)


def tokens_of(ref, half, side, start):
    pieces = []
    for head in range(16):
        pieces.append(ref[2 * head + half, start : start + 32, side * 64 : (side + 1) * 64])
    return jnp.concatenate(pieces, axis=1)


def join_kernel(folded, out):
    for half in range(2):
        for side in range(2):
            at = half * 64 + side * 32
            out[at : at + 32, :] = tokens_of(folded, half, side, 0)


def key_kernel(turned, dk_0, dk_1, dk_2, dk_3, out):
    dks = jnp.concatenate([dk_0[...], dk_1[...], dk_2[...], dk_3[...]], axis=0)
    total = dot(turned[...], dks)
    for block in range(64):
        out[block] = total[4 * block : 4 * block + 4].astype(BF)


def post_kernel(dk, folded, w_query, w_key, w_value, prefix_grad, latent_grad, dv, dq):
    @pl.when(pl.program_id(0) == 0)
    def _():
        for half in range(2):
            for side in range(2):
                at = half * 64 + side * 32
                dv[at : at + 32, :] = tokens_of(folded, half, side, 32)
        for side in range(2):
            pieces = []
            for head in range(16):
                part = [folded[2 * head + half, 64:80, side * 64 : (side + 1) * 64].astype(F32) for half in range(2)]
                pieces.append(part[0] + part[1])
            dq[side * 16 : (side + 1) * 16, :] = jnp.concatenate(pieces, axis=1).astype(BF)

    prefix_grad[...] = (dot_nt(dk[...], w_key[...]) + dot_nt(dv[...], w_value[...])).astype(BF)
    latent_grad[...] = dot_nt(dq[...], w_query[...]).astype(BF)


def call(kernel, out_shape, flops=0, nbytes=0, limit=24, **kwargs):
    return pl.pallas_call(
        kernel,
        out_shape=out_shape,
        compiler_params=pltpu.CompilerParams(vmem_limit_bytes=limit << 20),
        cost_estimate=pl.CostEstimate(flops=flops, bytes_accessed=nbytes, transcendentals=0),
        **kwargs,
    )


VMEM = pl.BlockSpec(memory_space=pltpu.VMEM)
SMEM = pl.BlockSpec(memory_space=pltpu.SMEM)
shape = jax.ShapeDtypeStruct


def whole(rows):
    return pl.BlockSpec((rows, 1024), lambda i: (0, 0))


def cols(rows):
    return pl.BlockSpec((rows, 256), lambda i: (0, i))


def wide(rows):
    return pl.BlockSpec((rows, 512), lambda i: (0, i))


def run_pre(prefix, latents, grad, saved, w_query, w_key, w_value):
    return call(
        pre_kernel,
        shape((32, 104, 128), BF),
        limit=60,
        flops=2 * 288 * 1024 * 1024,
        nbytes=8 << 20,
        grid=(2,),
        in_specs=[whole(128), whole(32), wide(32), wide(32), wide(1024), wide(1024), wide(1024)],
        out_specs=pl.BlockSpec((16, 104, 128), lambda i: (i, 0, 0)),
    )(prefix, latents, grad, saved, w_query, w_key, w_value)


def run_stats(half, vis_row, data):
    return call(
        stats_kernel,
        (shape((8, 1024), F32), shape((2, 1024, 1024), F32)),
        flops=2 * 1024 * 2048 * 64,
        nbytes=1 << 19,
        in_specs=[SMEM, VMEM, VMEM],
        out_specs=(VMEM, VMEM),
        scratch_shapes=[pltpu.VMEM((1024, 128), BF)] * 2,
    )(half, vis_row, data)


def run_dprobs(data):
    return call(
        dprobs_kernel,
        shape((2, 1024, 1024), F32),
        flops=2 * 1024 * 2048 * 64,
        nbytes=1 << 19,
        in_specs=[VMEM],
        out_specs=VMEM,
        scratch_shapes=[pltpu.VMEM((1024, 128), BF)] * 2 + [pltpu.VMEM((1, 1024), F32)],
    )(data)


def run_grad(data, scores, dprobs, stats, other):
    return call(
        grad_kernel,
        shape((32, 80, 128), BF),
        flops=6 * 1024 * 2048 * 64,
        nbytes=1 << 20,
        in_specs=[VMEM] * 5,
        out_specs=VMEM,
        scratch_shapes=[pltpu.VMEM((1024, 128), BF)] * 4
        + [
            pltpu.VMEM((CHUNKS, DH, SRC_CHUNK * 64), BF),
            pltpu.VMEM((1024, 128), F32),
            pltpu.VMEM((1024, 128), F32),
        ],
    )(data, scores, dprobs, stats, other)


def run_join(back):
    return call(join_kernel, shape((128, 1024), BF), nbytes=1 << 19, in_specs=[VMEM], out_specs=VMEM)(back)


def run_key(turned, *dks):
    return call(
        key_kernel,
        shape((64, 4, 1024), BF),
        flops=2 * 256 * 512 * 1024,
        nbytes=2 << 20,
        in_specs=[VMEM] * 5,
        out_specs=VMEM,
    )(turned, *dks)


def run_post(dk, back, w_query, w_key, w_value):
    rows = pl.BlockSpec((256, 1024), lambda i: (i, 0))
    return call(
        post_kernel,
        (shape((128, 1024), BF), shape((32, 1024), BF)),
        limit=60,
        flops=2 * 288 * 1024 * 1024,
        nbytes=8 << 20,
        grid=(4,),
        in_specs=[whole(128), pl.BlockSpec((32, 80, 128), lambda i: (0, 0, 0))] + [rows] * 3,
        out_specs=(cols(128), cols(32)),
        scratch_shapes=[pltpu.VMEM((128, 1024), BF), pltpu.VMEM((32, 1024), BF)],
    )(dk, back, w_query, w_key, w_value)


def pick_rows(x_high, core):
    at = lax.broadcasted_iota(jnp.int32, (1024, 1024), 0)
    x_to, core_to = x_high ^ (at >> 9), core ^ ((at >> 8) & 1)
    wanted = ((at >> 3) & 31) * 32 + x_to * 16 + ((at >> 2) & 1) * 8 + core_to * 4 + (at & 3)
    return (wanted == lax.broadcasted_iota(jnp.int32, (1024, 1024), 1)).astype(BF)


def on_device(prefix, latents, saved, grad, visible, w_query, w_key, w_value):
    prefix, latents, saved, grad = prefix[0], latents[0], saved[0], grad[0]
    half = jnp.reshape(lax.axis_index("z") % 2, (1,)).astype(jnp.int32)
    over_core = lambda v: lax.ppermute(v, "core", [(0, 1), (1, 0)])
    over_x = lambda v: lax.ppermute(v, "x_high", [(0, 1), (1, 0)])

    data = run_pre(prefix, latents, grad, saved, w_query, w_key, w_value)
    data = lax.all_to_all(data, ("y", "z"), 0, 0, tiled=True)
    picked = pick_rows(lax.axis_index("x_high"), lax.axis_index("core"))
    turned = dot_nt(picked, prefix).astype(BF).reshape(4, 256, 128)
    gained = over_core(jnp.stack([turned[1], turned[3]]))
    far_t = over_x(jnp.stack([turned[2], gained[1]]))
    turned = jnp.concatenate([turned[0], gained[0], far_t[0], far_t[1]], axis=1)

    stats, scores = run_stats(half, visible, data)
    stats, turned = lax.optimization_barrier((stats, turned))
    other = lax.ppermute(stats, "z", [(i, i ^ 1) for i in range(8)])
    dprobs = run_dprobs(data)
    back = run_grad(data, scores, dprobs, stats, other)
    back = lax.all_to_all(back, ("y", "z"), 0, 0, tiled=True)

    dk = run_join(back)
    far_dk = over_x(dk)
    part = run_key(turned, dk, over_core(dk), far_dk, over_core(far_dk))
    part = lax.all_to_all(part, ("y", "z", "x_low"), 0, 0, tiled=True)
    key_wgrad = jnp.sum(part.astype(F32), axis=0)
    prefix_grad, latent_grad = run_post(dk, back, w_query, w_key, w_value)
    return prefix_grad[None], latent_grad[None], key_wgrad


def solution(mesh):
    grid = Mesh(mesh.devices.reshape(4, 8, 2, 2, 2), ("y", "z", "x_high", "x_low", "core"))
    seq, dp = ("y", "z"), ("x_high", "x_low", "core")
    return jax.shard_map(
        on_device,
        mesh=grid,
        in_specs=(
            P(dp, seq, None),
            P(dp, seq, None),
            P(dp, seq, None),
            P(dp, seq, None),
            P(dp, None),
            P(),
            P(),
            P(),
        ),
        out_specs=(P(dp, seq, None), P(dp, seq, None), P(seq + dp, None)),
        check_vma=False,
    )
```

```python
import functools
import math

import jax
import jax.numpy as jnp
from jax import lax
from jax.experimental import pallas as pl
from jax.experimental.pallas import tpu as pltpu
from jax.sharding import Mesh, PartitionSpec as P

BF = jnp.bfloat16
F32 = jnp.float32
DH = 64
NEG = -1e30
FLOOR = -1e29
SCALE = 1.0 / math.sqrt(DH)
C = SCALE * math.log2(math.e)
NT_DIMS = (((1,), (1,)), ((), ()))
LAT_TILE = 512
SRC_CHUNK = 16


def dot(a, b):
    return jnp.dot(a, b, preferred_element_type=F32)


def dot_nt(a, b):
    return lax.dot_general(a, b, NT_DIMS, preferred_element_type=F32)


def swap(x):
    return jnp.concatenate([x[..., 64:], x[..., :64]], axis=-1)


def fold(x, rows):
    return jnp.concatenate([x[:rows], x[rows:]], axis=1)


def pre_kernel(prefix, latents, grad, saved, w_query, w_key, w_value, out):
    keys = dot(prefix[...], w_key[...]).astype(BF)
    values = dot(prefix[...], w_value[...]).astype(BF)
    queries = dot(latents[...], w_query[...]).astype(BF)
    g = grad[...]
    product = g.astype(F32) * saved[...].astype(F32)
    product = jnp.concatenate([product, jnp.zeros((96, product.shape[1]), F32)], axis=0).T
    row = lax.broadcasted_iota(jnp.int32, (8, 128), 0)
    for head in range(8):
        cols = slice(head * DH, (head + 1) * DH)
        delta = jnp.sum(product[cols], axis=0, keepdims=True)
        high = delta.astype(BF).astype(F32)
        mid = (delta - high).astype(BF).astype(F32)
        low = delta - high - mid
        parts = jnp.where(row == 0, high, jnp.where(row == 1, mid, jnp.where(row == 2, low, 0.0)))
        q_fold = fold(queries[:, cols], 16)
        g_fold = fold(g[:, cols], 16)
        for half in range(2):
            toks = slice(half * 64, (half + 1) * 64)
            dest = 2 * head + half
            out[dest, 0:32, :] = fold(keys[toks, cols], 32)
            out[dest, 32:64, :] = fold(values[toks, cols], 32)
            out[dest, 64:80, :] = q_fold
            out[dest, 80:96, :] = g_fold
            out[dest, 96:104, :] = parts.astype(BF)


def unfold(folded, low_ref, high_ref):
    lane = lax.broadcasted_iota(jnp.int32, folded.shape, 2)
    other = swap(folded)
    zero = jnp.zeros_like(folded)
    left = lane < 64
    low = jnp.concatenate([jnp.where(left, folded, zero), jnp.where(left, other, zero)], axis=1)
    high = jnp.concatenate([jnp.where(left, zero, other), jnp.where(left, zero, folded)], axis=1)
    low_ref[...] = low.reshape(low_ref.shape)
    high_ref[...] = high.reshape(high_ref.shape)


SPAN = SRC_CHUNK * 128
ROWS = SRC_CHUNK * 32
CHUNKS = 32 // SRC_CHUNK


def hide(scores, bound):
    parts = scores.reshape(SRC_CHUNK, 32, LAT_TILE)
    row = lax.broadcasted_iota(jnp.int32, (1, 32, LAT_TILE), 1)
    first = lax.broadcasted_iota(jnp.int32, (SRC_CHUNK, 1, LAT_TILE), 0) * 128
    return jnp.where(row < bound[None] - first, parts, NEG).reshape(ROWS, LAT_TILE)


def all_chunks(step, carry):
    for chunk in range(CHUNKS):
        carry = step(chunk, carry)
    return carry


def stats_kernel(half_s, vis, data, out, scores, q_low, q_high):
    half = half_s[0]
    unfold(data[:, 64:80, :], q_low, q_high)
    for tile in range(1024 // LAT_TILE):
        lanes = slice(tile * LAT_TILE, (tile + 1) * LAT_TILE)
        seen = vis[:, lanes] - half * 64
        ql = q_low[lanes, :]
        qh = q_high[lanes, :]

        def step(chunk, carry):
            top, total = carry
            k = data[slice(chunk * SRC_CHUNK, (chunk + 1) * SRC_CHUNK), 0:32, :].reshape(ROWS, 128)
            s_low = hide(dot_nt(k, ql), seen - chunk * SPAN)
            s_high = hide(dot_nt(k, qh), seen - 32 - chunk * SPAN)
            place = slice(chunk * ROWS, (chunk + 1) * ROWS)
            scores[0, place, lanes] = s_low
            scores[1, place, lanes] = s_high
            new = jnp.max(jnp.maximum(s_low, s_high), axis=0, keepdims=True)
            new = jnp.maximum(new, top)
            part = jnp.sum(jnp.exp2((s_low - new) * C) + jnp.exp2((s_high - new) * C), axis=0, keepdims=True)
            return new, total * jnp.exp2((top - new) * C) + part

        start = (jnp.full((1, LAT_TILE), FLOOR, F32), jnp.zeros((1, LAT_TILE), F32))
        top, total = all_chunks(step, start)
        out[0:1, lanes] = top
        out[1:2, lanes] = total
    out[2:8, :] = jnp.zeros((6, 1024), F32)


def dprobs_kernel(data, out, q_low, q_high, g_low, g_high, k_t, delta_ref):
    unfold(data[:, 64:80, :], q_low, q_high)
    unfold(data[:, 80:96, :], g_low, g_high)
    for chunk in range(CHUNKS):
        k = data[chunk * SRC_CHUNK : (chunk + 1) * SRC_CHUNK, 0:32, :].reshape(ROWS, 128)
        turned = k.T
        k_t[chunk] = jnp.concatenate([turned[0:64], turned[64:128]], axis=1)
    lane = lax.broadcasted_iota(jnp.int32, (1, 128), 1)
    for block in range(8):
        joined = jnp.zeros((1, 128), F32)
        for place in range(4):
            parts = data[4 * block + place, 96:104, :].astype(F32)
            parts = jnp.sum(parts, axis=0, keepdims=True)
            if place:
                parts = pltpu.roll(parts, 32 * place, 1)
            joined = jnp.where((lane >> 5) == place, parts, joined)
        delta_ref[:, block * 128 : (block + 1) * 128] = joined
    for chunk in range(CHUNKS):
        place = slice(chunk * ROWS, (chunk + 1) * ROWS)
        v = data[chunk * SRC_CHUNK : (chunk + 1) * SRC_CHUNK, 32:64, :].reshape(ROWS, 128)
        for tile in range(1024 // LAT_TILE):
            lanes = slice(tile * LAT_TILE, (tile + 1) * LAT_TILE)
            out[0, place, lanes] = dot_nt(v, g_low[lanes, :]) - delta_ref[:, lanes]
            out[1, place, lanes] = dot_nt(v, g_high[lanes, :]) - delta_ref[:, lanes]


def grad_kernel(scores, dprobs, q_low, q_high, g_low, g_high, k_t, own, other, out, dk_acc, dv_acc):
    dk_acc[...] = jnp.zeros_like(dk_acc)
    dv_acc[...] = jnp.zeros_like(dv_acc)
    top = jnp.maximum(own[0:1, :], other[0:1, :])
    total = own[1:2, :] * jnp.exp2((own[0:1, :] - top) * C) + other[1:2, :] * jnp.exp2((other[0:1, :] - top) * C)
    lse = top + jnp.log2(total) * (1.0 / C)
    for tile in range(1024 // LAT_TILE):
        lanes = slice(tile * LAT_TILE, (tile + 1) * LAT_TILE)
        lse_t = lse[:, lanes]
        ql, qh, gl, gh = q_low[lanes, :], q_high[lanes, :], g_low[lanes, :], g_high[lanes, :]

        def step(chunk, dq):
            place = slice(chunk * ROWS, (chunk + 1) * ROWS)
            p_low = jnp.exp2((scores[0, place, lanes] - lse_t) * C)
            p_high = jnp.exp2((scores[1, place, lanes] - lse_t) * C)
            ds_low = (p_low * dprobs[0, place, lanes]).astype(BF)
            ds_high = (p_high * dprobs[1, place, lanes]).astype(BF)
            dv_acc[place, :] += dot(p_low.astype(BF), gl) + dot(p_high.astype(BF), gh)
            dk_acc[place, :] += dot(ds_low, ql) + dot(ds_high, qh)
            return dq + dot(k_t[chunk], jnp.concatenate([ds_low, ds_high], axis=0))

        dq = all_chunks(step, jnp.zeros((DH, LAT_TILE), F32))
        dq = (dq * SCALE).T
        for block in range(LAT_TILE // 32):
            part = dq[block * 32 : (block + 1) * 32]
            out[tile * (LAT_TILE // 32) + block, 64:80, :] = fold(part, 16).astype(BF)
    out[:, 0:32, :] = (dk_acc[...] * SCALE).astype(BF).reshape(32, 32, 128)
    out[:, 32:64, :] = dv_acc[...].astype(BF).reshape(32, 32, 128)


def tokens_of(ref, half, side, start):
    pieces = []
    for head in range(16):
        pieces.append(ref[2 * head + half, start : start + 32, side * 64 : (side + 1) * 64])
    return jnp.concatenate(pieces, axis=1)


def join_kernel(folded, out):
    for half in range(2):
        for side in range(2):
            at = half * 64 + side * 32
            out[at : at + 32, :] = tokens_of(folded, half, side, 0)


def key_kernel(turned, dk_0, dk_1, dk_2, dk_3, out):
    dks = jnp.concatenate([dk_0[...], dk_1[...], dk_2[...], dk_3[...]], axis=0)
    total = dot(turned[...], dks)
    for block in range(64):
        out[block] = total[4 * block : 4 * block + 4].astype(BF)


def post_kernel(dk, folded, w_query, w_key, w_value, prefix_grad, latent_grad, dv, dq):
    @pl.when(pl.program_id(0) == 0)
    def _():
        for half in range(2):
            for side in range(2):
                at = half * 64 + side * 32
                dv[at : at + 32, :] = tokens_of(folded, half, side, 32)
        for side in range(2):
            pieces = []
            for head in range(16):
                part = [folded[2 * head + half, 64:80, side * 64 : (side + 1) * 64].astype(F32) for half in range(2)]
                pieces.append(part[0] + part[1])
            dq[side * 16 : (side + 1) * 16, :] = jnp.concatenate(pieces, axis=1).astype(BF)

    prefix_grad[...] = (dot_nt(dk[...], w_key[...]) + dot_nt(dv[...], w_value[...])).astype(BF)
    latent_grad[...] = dot_nt(dq[...], w_query[...]).astype(BF)


def call(kernel, out_shape, flops=0, nbytes=0, limit=24, **kwargs):
    return pl.pallas_call(
        kernel,
        out_shape=out_shape,
        compiler_params=pltpu.CompilerParams(vmem_limit_bytes=limit << 20),
        cost_estimate=pl.CostEstimate(flops=flops, bytes_accessed=nbytes, transcendentals=0),
        **kwargs,
    )


VMEM = pl.BlockSpec(memory_space=pltpu.VMEM)
SMEM = pl.BlockSpec(memory_space=pltpu.SMEM)
shape = jax.ShapeDtypeStruct


def whole(rows):
    return pl.BlockSpec((rows, 1024), lambda i: (0, 0))


def cols(rows):
    return pl.BlockSpec((rows, 256), lambda i: (0, i))


def wide(rows):
    return pl.BlockSpec((rows, 512), lambda i: (0, i))


def run_pre(prefix, latents, grad, saved, w_query, w_key, w_value):
    return call(
        pre_kernel,
        shape((32, 104, 128), BF),
        limit=60,
        flops=2 * 288 * 1024 * 1024,
        nbytes=8 << 20,
        grid=(2,),
        in_specs=[whole(128), whole(32), wide(32), wide(32), wide(1024), wide(1024), wide(1024)],
        out_specs=pl.BlockSpec((16, 104, 128), lambda i: (i, 0, 0)),
    )(prefix, latents, grad, saved, w_query, w_key, w_value)


def run_stats(half, vis_row, data):
    return call(
        stats_kernel,
        (shape((8, 1024), F32), shape((2, 1024, 1024), F32)),
        flops=2 * 1024 * 2048 * 64,
        nbytes=1 << 19,
        in_specs=[SMEM, VMEM, VMEM],
        out_specs=(VMEM, VMEM),
        scratch_shapes=[pltpu.VMEM((1024, 128), BF)] * 2,
    )(half, vis_row, data)


def run_dprobs(data):
    return call(
        dprobs_kernel,
        (shape((2, 1024, 1024), F32),)
        + (shape((1024, 128), BF),) * 4
        + (shape((CHUNKS, DH, SRC_CHUNK * 64), BF),),
        flops=2 * 1024 * 2048 * 64,
        nbytes=1 << 19,
        in_specs=[VMEM],
        out_specs=(VMEM,) * 6,
        scratch_shapes=[pltpu.VMEM((1, 1024), F32)],
    )(data)


def run_grad(scores, local, stats, other):
    return call(
        grad_kernel,
        shape((32, 80, 128), BF),
        flops=6 * 1024 * 2048 * 64,
        nbytes=1 << 20,
        in_specs=[VMEM] * 9,
        out_specs=VMEM,
        scratch_shapes=[pltpu.VMEM((1024, 128), F32)] * 2,
    )(scores, *local, stats, other)


def run_join(back):
    return call(join_kernel, shape((128, 1024), BF), nbytes=1 << 19, in_specs=[VMEM], out_specs=VMEM)(back)


def run_key(turned, *dks):
    return call(
        key_kernel,
        shape((64, 4, 1024), BF),
        flops=2 * 256 * 512 * 1024,
        nbytes=2 << 20,
        in_specs=[VMEM] * 5,
        out_specs=VMEM,
    )(turned, *dks)


def run_post(dk, back, w_query, w_key, w_value):
    rows = pl.BlockSpec((256, 1024), lambda i: (i, 0))
    return call(
        post_kernel,
        (shape((128, 1024), BF), shape((32, 1024), BF)),
        limit=60,
        flops=2 * 288 * 1024 * 1024,
        nbytes=8 << 20,
        grid=(4,),
        in_specs=[whole(128), pl.BlockSpec((32, 80, 128), lambda i: (0, 0, 0))] + [rows] * 3,
        out_specs=(cols(128), cols(32)),
        scratch_shapes=[pltpu.VMEM((128, 1024), BF), pltpu.VMEM((32, 1024), BF)],
    )(dk, back, w_query, w_key, w_value)


def pick_rows(x_high, core):
    at = lax.broadcasted_iota(jnp.int32, (1024, 1024), 0)
    x_to, core_to = x_high ^ (at >> 9), core ^ ((at >> 8) & 1)
    wanted = ((at >> 3) & 31) * 32 + x_to * 16 + ((at >> 2) & 1) * 8 + core_to * 4 + (at & 3)
    return (wanted == lax.broadcasted_iota(jnp.int32, (1024, 1024), 1)).astype(BF)


def on_device(prefix, latents, saved, grad, visible, w_query, w_key, w_value):
    prefix, latents, saved, grad = prefix[0], latents[0], saved[0], grad[0]
    half = jnp.reshape(lax.axis_index("z") % 2, (1,)).astype(jnp.int32)
    over_core = lambda v: lax.ppermute(v, "core", [(0, 1), (1, 0)])
    over_x = lambda v: lax.ppermute(v, "x_high", [(0, 1), (1, 0)])

    data = run_pre(prefix, latents, grad, saved, w_query, w_key, w_value)
    data = lax.all_to_all(data, ("y", "z"), 0, 0, tiled=True)
    picked = pick_rows(lax.axis_index("x_high"), lax.axis_index("core"))
    turned = dot_nt(picked, prefix).astype(BF).reshape(4, 256, 128)
    gained = over_core(jnp.stack([turned[1], turned[3]]))
    far_t = over_x(jnp.stack([turned[2], gained[1]]))
    turned = jnp.concatenate([turned[0], gained[0], far_t[0], far_t[1]], axis=1)

    stats, scores = run_stats(half, visible, data)
    stats, turned = lax.optimization_barrier((stats, turned))
    other = lax.ppermute(stats, "z", [(i, i ^ 1) for i in range(8)])
    back = run_grad(scores, run_dprobs(data), stats, other)
    back = lax.all_to_all(back, ("y", "z"), 0, 0, tiled=True)

    dk = run_join(back)
    far_dk = over_x(dk)
    part = run_key(turned, dk, over_core(dk), far_dk, over_core(far_dk))
    part = lax.all_to_all(part, ("y", "z", "x_low"), 0, 0, tiled=True)
    key_wgrad = jnp.sum(part.astype(F32), axis=0)
    prefix_grad, latent_grad = run_post(dk, back, w_query, w_key, w_value)
    return prefix_grad[None], latent_grad[None], key_wgrad


def solution(mesh):
    grid = Mesh(mesh.devices.reshape(4, 8, 2, 2, 2), ("y", "z", "x_high", "x_low", "core"))
    seq, dp = ("y", "z"), ("x_high", "x_low", "core")
    return jax.shard_map(
        on_device,
        mesh=grid,
        in_specs=(
            P(dp, seq, None),
            P(dp, seq, None),
            P(dp, seq, None),
            P(dp, seq, None),
            P(dp, None),
            P(),
            P(),
            P(),
        ),
        out_specs=(P(dp, seq, None), P(dp, seq, None), P(seq + dp, None)),
        check_vma=False,
    )
```

```python
import functools
import math

import jax
import jax.numpy as jnp
from jax import lax
from jax.experimental import pallas as pl
from jax.experimental.pallas import tpu as pltpu
from jax.sharding import Mesh, PartitionSpec as P

BF = jnp.bfloat16
F32 = jnp.float32
DH = 64
NEG = -1e30
FLOOR = -1e29
SCALE = 1.0 / math.sqrt(DH)
C = SCALE * math.log2(math.e)
NT_DIMS = (((1,), (1,)), ((), ()))
LAT_TILE = 512
SRC_CHUNK = 16


def dot(a, b):
    return jnp.dot(a, b, preferred_element_type=F32)


def dot_nt(a, b):
    return lax.dot_general(a, b, NT_DIMS, preferred_element_type=F32)


def swap(x):
    return jnp.concatenate([x[..., 64:], x[..., :64]], axis=-1)


def fold(x, rows):
    return jnp.concatenate([x[:rows], x[rows:]], axis=1)


def pre_kernel(prefix, latents, grad, saved, w_query, w_key, w_value, out):
    keys = dot(prefix[...], w_key[...]).astype(BF)
    values = dot(prefix[...], w_value[...]).astype(BF)
    queries = dot(latents[...], w_query[...]).astype(BF)
    g = grad[...]
    product = g.astype(F32) * saved[...].astype(F32)
    product = jnp.concatenate([product, jnp.zeros((96, product.shape[1]), F32)], axis=0).T
    row = lax.broadcasted_iota(jnp.int32, (8, 128), 0)
    for head in range(8):
        cols = slice(head * DH, (head + 1) * DH)
        delta = jnp.sum(product[cols], axis=0, keepdims=True)
        high = delta.astype(BF).astype(F32)
        mid = (delta - high).astype(BF).astype(F32)
        low = delta - high - mid
        parts = jnp.where(row == 0, high, jnp.where(row == 1, mid, jnp.where(row == 2, low, 0.0)))
        q_fold = fold(queries[:, cols], 16)
        g_fold = fold(g[:, cols], 16)
        for half in range(2):
            toks = slice(half * 64, (half + 1) * 64)
            dest = 2 * head + half
            out[dest, 0:32, :] = fold(keys[toks, cols], 32)
            out[dest, 32:64, :] = fold(values[toks, cols], 32)
            out[dest, 64:80, :] = q_fold
            out[dest, 80:96, :] = g_fold
            out[dest, 96:104, :] = parts.astype(BF)


def unfold(folded, low_ref, high_ref):
    lane = lax.broadcasted_iota(jnp.int32, folded.shape, 2)
    other = swap(folded)
    zero = jnp.zeros_like(folded)
    left = lane < 64
    low = jnp.concatenate([jnp.where(left, folded, zero), jnp.where(left, other, zero)], axis=1)
    high = jnp.concatenate([jnp.where(left, zero, other), jnp.where(left, zero, folded)], axis=1)
    low_ref[...] = low.reshape(low_ref.shape)
    high_ref[...] = high.reshape(high_ref.shape)


SPAN = SRC_CHUNK * 128
ROWS = SRC_CHUNK * 32
CHUNKS = 32 // SRC_CHUNK


def hide(scores, bound):
    parts = scores.reshape(SRC_CHUNK, 32, LAT_TILE)
    row = lax.broadcasted_iota(jnp.int32, (1, 32, LAT_TILE), 1)
    first = lax.broadcasted_iota(jnp.int32, (SRC_CHUNK, 1, LAT_TILE), 0) * 128
    return jnp.where(row < bound[None] - first, parts, NEG).reshape(ROWS, LAT_TILE)


def all_chunks(step, carry):
    for chunk in range(CHUNKS):
        carry = step(chunk, carry)
    return carry


def stats_kernel(half_s, vis, data, out, scores, q_low, q_high):
    half = half_s[0]
    unfold(data[:, 64:80, :], q_low, q_high)
    for tile in range(1024 // LAT_TILE):
        lanes = slice(tile * LAT_TILE, (tile + 1) * LAT_TILE)
        seen = vis[:, lanes] - half * 64
        ql = q_low[lanes, :]
        qh = q_high[lanes, :]

        def step(chunk, carry):
            top, total = carry
            k = data[slice(chunk * SRC_CHUNK, (chunk + 1) * SRC_CHUNK), 0:32, :].reshape(ROWS, 128)
            s_low = hide(dot_nt(k, ql), seen - chunk * SPAN)
            s_high = hide(dot_nt(k, qh), seen - 32 - chunk * SPAN)
            place = slice(chunk * ROWS, (chunk + 1) * ROWS)
            scores[0, place, lanes] = s_low
            scores[1, place, lanes] = s_high
            new = jnp.max(jnp.maximum(s_low, s_high), axis=0, keepdims=True)
            new = jnp.maximum(new, top)
            part = jnp.sum(jnp.exp2((s_low - new) * C) + jnp.exp2((s_high - new) * C), axis=0, keepdims=True)
            return new, total * jnp.exp2((top - new) * C) + part

        start = (jnp.full((1, LAT_TILE), FLOOR, F32), jnp.zeros((1, LAT_TILE), F32))
        top, total = all_chunks(step, start)
        out[0:1, lanes] = top
        out[1:2, lanes] = total
    out[2:8, :] = jnp.zeros((6, 1024), F32)


def dprobs_kernel(data, out, q_low, q_high, g_low, g_high, k_t, delta_ref):
    unfold(data[:, 64:80, :], q_low, q_high)
    unfold(data[:, 80:96, :], g_low, g_high)
    for chunk in range(CHUNKS):
        k = data[chunk * SRC_CHUNK : (chunk + 1) * SRC_CHUNK, 0:32, :].reshape(ROWS, 128)
        turned = k.T
        k_t[chunk] = jnp.concatenate([turned[0:64], turned[64:128]], axis=1)
    lane = lax.broadcasted_iota(jnp.int32, (1, 128), 1)
    for block in range(8):
        joined = jnp.zeros((1, 128), F32)
        for place in range(4):
            parts = data[4 * block + place, 96:104, :].astype(F32)
            parts = jnp.sum(parts, axis=0, keepdims=True)
            if place:
                parts = pltpu.roll(parts, 32 * place, 1)
            joined = jnp.where((lane >> 5) == place, parts, joined)
        delta_ref[:, block * 128 : (block + 1) * 128] = joined
    for chunk in range(CHUNKS):
        place = slice(chunk * ROWS, (chunk + 1) * ROWS)
        v = data[chunk * SRC_CHUNK : (chunk + 1) * SRC_CHUNK, 32:64, :].reshape(ROWS, 128)
        for tile in range(1024 // LAT_TILE):
            lanes = slice(tile * LAT_TILE, (tile + 1) * LAT_TILE)
            out[0, place, lanes] = dot_nt(v, g_low[lanes, :]) - delta_ref[:, lanes]
            out[1, place, lanes] = dot_nt(v, g_high[lanes, :]) - delta_ref[:, lanes]


def grad_kernel(scores, dprobs, q_low, q_high, g_low, g_high, k_t, own, other, out, dk_acc, dv_acc):
    top = jnp.maximum(own[0:1, :], other[0:1, :])
    total = own[1:2, :] * jnp.exp2((own[0:1, :] - top) * C) + other[1:2, :] * jnp.exp2((other[0:1, :] - top) * C)
    lse = top + jnp.log2(total) * (1.0 / C)
    for tile in range(1024 // LAT_TILE):
        lanes = slice(tile * LAT_TILE, (tile + 1) * LAT_TILE)
        lse_t = lse[:, lanes]
        ql, qh, gl, gh = q_low[lanes, :], q_high[lanes, :], g_low[lanes, :], g_high[lanes, :]

        def step(chunk, dq):
            place = slice(chunk * ROWS, (chunk + 1) * ROWS)
            p_low = jnp.exp2((scores[0, place, lanes] - lse_t) * C)
            p_high = jnp.exp2((scores[1, place, lanes] - lse_t) * C)
            ds_low = (p_low * dprobs[0, place, lanes]).astype(BF)
            ds_high = (p_high * dprobs[1, place, lanes]).astype(BF)
            dv = dot(p_low.astype(BF), gl) + dot(p_high.astype(BF), gh)
            dk = dot(ds_low, ql) + dot(ds_high, qh)
            dv_acc[place, :] = dv_acc[place, :] + dv if tile else dv
            dk_acc[place, :] = dk_acc[place, :] + dk if tile else dk
            return dq + dot(k_t[chunk], jnp.concatenate([ds_low, ds_high], axis=0))

        dq = all_chunks(step, jnp.zeros((DH, LAT_TILE), F32))
        dq = (dq * SCALE).T
        for block in range(LAT_TILE // 32):
            part = dq[block * 32 : (block + 1) * 32]
            out[tile * (LAT_TILE // 32) + block, 64:80, :] = fold(part, 16).astype(BF)
    out[:, 0:32, :] = (dk_acc[...] * SCALE).astype(BF).reshape(32, 32, 128)
    out[:, 32:64, :] = dv_acc[...].astype(BF).reshape(32, 32, 128)


def tokens_of(ref, half, side, start):
    pieces = []
    for head in range(16):
        pieces.append(ref[2 * head + half, start : start + 32, side * 64 : (side + 1) * 64])
    return jnp.concatenate(pieces, axis=1)


def join_kernel(folded, out):
    for half in range(2):
        for side in range(2):
            at = half * 64 + side * 32
            out[at : at + 32, :] = tokens_of(folded, half, side, 0)


def key_kernel(turned, dk_0, dk_1, dk_2, dk_3, out):
    dks = jnp.concatenate([dk_0[...], dk_1[...], dk_2[...], dk_3[...]], axis=0)
    total = dot(turned[...], dks)
    for block in range(64):
        out[block] = total[4 * block : 4 * block + 4].astype(BF)


def post_kernel(dk, folded, w_query, w_key, w_value, prefix_grad, latent_grad, dv, dq):
    @pl.when(pl.program_id(0) == 0)
    def _():
        for half in range(2):
            for side in range(2):
                at = half * 64 + side * 32
                dv[at : at + 32, :] = tokens_of(folded, half, side, 32)
        for side in range(2):
            pieces = []
            for head in range(16):
                part = [folded[2 * head + half, 64:80, side * 64 : (side + 1) * 64].astype(F32) for half in range(2)]
                pieces.append(part[0] + part[1])
            dq[side * 16 : (side + 1) * 16, :] = jnp.concatenate(pieces, axis=1).astype(BF)

    prefix_grad[...] = (dot_nt(dk[...], w_key[...]) + dot_nt(dv[...], w_value[...])).astype(BF)
    latent_grad[...] = dot_nt(dq[...], w_query[...]).astype(BF)


def call(kernel, out_shape, flops=0, nbytes=0, limit=24, **kwargs):
    return pl.pallas_call(
        kernel,
        out_shape=out_shape,
        compiler_params=pltpu.CompilerParams(vmem_limit_bytes=limit << 20),
        cost_estimate=pl.CostEstimate(flops=flops, bytes_accessed=nbytes, transcendentals=0),
        **kwargs,
    )


VMEM = pl.BlockSpec(memory_space=pltpu.VMEM)
SMEM = pl.BlockSpec(memory_space=pltpu.SMEM)
shape = jax.ShapeDtypeStruct


def whole(rows):
    return pl.BlockSpec((rows, 1024), lambda i: (0, 0))


def cols(rows):
    return pl.BlockSpec((rows, 256), lambda i: (0, i))


def wide(rows):
    return pl.BlockSpec((rows, 512), lambda i: (0, i))


def run_pre(prefix, latents, grad, saved, w_query, w_key, w_value):
    return call(
        pre_kernel,
        shape((32, 104, 128), BF),
        limit=60,
        flops=2 * 288 * 1024 * 1024,
        nbytes=8 << 20,
        grid=(2,),
        in_specs=[whole(128), whole(32), wide(32), wide(32), wide(1024), wide(1024), wide(1024)],
        out_specs=pl.BlockSpec((16, 104, 128), lambda i: (i, 0, 0)),
    )(prefix, latents, grad, saved, w_query, w_key, w_value)


def run_stats(half, vis_row, data):
    return call(
        stats_kernel,
        (shape((8, 1024), F32), shape((2, 1024, 1024), F32)),
        flops=2 * 1024 * 2048 * 64,
        nbytes=1 << 19,
        in_specs=[SMEM, VMEM, VMEM],
        out_specs=(VMEM, VMEM),
        scratch_shapes=[pltpu.VMEM((1024, 128), BF)] * 2,
    )(half, vis_row, data)


def run_dprobs(data):
    return call(
        dprobs_kernel,
        (shape((2, 1024, 1024), F32),)
        + (shape((1024, 128), BF),) * 4
        + (shape((CHUNKS, DH, SRC_CHUNK * 64), BF),),
        flops=2 * 1024 * 2048 * 64,
        nbytes=1 << 19,
        in_specs=[VMEM],
        out_specs=(VMEM,) * 6,
        scratch_shapes=[pltpu.VMEM((1, 1024), F32)],
    )(data)


def run_grad(scores, local, stats, other):
    return call(
        grad_kernel,
        shape((32, 80, 128), BF),
        flops=6 * 1024 * 2048 * 64,
        nbytes=1 << 20,
        in_specs=[VMEM] * 9,
        out_specs=VMEM,
        scratch_shapes=[pltpu.VMEM((1024, 128), F32)] * 2,
    )(scores, *local, stats, other)


def run_join(back):
    return call(join_kernel, shape((128, 1024), BF), nbytes=1 << 19, in_specs=[VMEM], out_specs=VMEM)(back)


def run_key(turned, *dks):
    return call(
        key_kernel,
        shape((64, 4, 1024), BF),
        flops=2 * 256 * 512 * 1024,
        nbytes=2 << 20,
        in_specs=[VMEM] * 5,
        out_specs=VMEM,
    )(turned, *dks)


def run_post(dk, back, w_query, w_key, w_value):
    rows = pl.BlockSpec((256, 1024), lambda i: (i, 0))
    return call(
        post_kernel,
        (shape((128, 1024), BF), shape((32, 1024), BF)),
        limit=60,
        flops=2 * 288 * 1024 * 1024,
        nbytes=8 << 20,
        grid=(4,),
        in_specs=[whole(128), pl.BlockSpec((32, 80, 128), lambda i: (0, 0, 0))] + [rows] * 3,
        out_specs=(cols(128), cols(32)),
        scratch_shapes=[pltpu.VMEM((128, 1024), BF), pltpu.VMEM((32, 1024), BF)],
    )(dk, back, w_query, w_key, w_value)


def pick_rows(x_high, core):
    at = lax.broadcasted_iota(jnp.int32, (1024, 1024), 0)
    x_to, core_to = x_high ^ (at >> 9), core ^ ((at >> 8) & 1)
    wanted = ((at >> 3) & 31) * 32 + x_to * 16 + ((at >> 2) & 1) * 8 + core_to * 4 + (at & 3)
    return (wanted == lax.broadcasted_iota(jnp.int32, (1024, 1024), 1)).astype(BF)


def on_device(prefix, latents, saved, grad, visible, w_query, w_key, w_value):
    prefix, latents, saved, grad = prefix[0], latents[0], saved[0], grad[0]
    half = jnp.reshape(lax.axis_index("z") % 2, (1,)).astype(jnp.int32)
    over_core = lambda v: lax.ppermute(v, "core", [(0, 1), (1, 0)])
    over_x = lambda v: lax.ppermute(v, "x_high", [(0, 1), (1, 0)])

    data = run_pre(prefix, latents, grad, saved, w_query, w_key, w_value)
    data = lax.all_to_all(data, ("y", "z"), 0, 0, tiled=True)
    picked = pick_rows(lax.axis_index("x_high"), lax.axis_index("core"))
    turned = dot_nt(picked, prefix).astype(BF).reshape(4, 256, 128)
    gained = over_core(jnp.stack([turned[1], turned[3]]))
    far_t = over_x(jnp.stack([turned[2], gained[1]]))
    turned = jnp.concatenate([turned[0], gained[0], far_t[0], far_t[1]], axis=1)

    stats, scores = run_stats(half, visible, data)
    stats, turned = lax.optimization_barrier((stats, turned))
    other = lax.ppermute(stats, "z", [(i, i ^ 1) for i in range(8)])
    back = run_grad(scores, run_dprobs(data), stats, other)
    back = lax.all_to_all(back, ("y", "z"), 0, 0, tiled=True)

    dk = run_join(back)
    far_dk = over_x(dk)
    part = run_key(turned, dk, over_core(dk), far_dk, over_core(far_dk))
    part = lax.all_to_all(part, ("y", "z", "x_low"), 0, 0, tiled=True)
    key_wgrad = jnp.sum(part.astype(F32), axis=0)
    prefix_grad, latent_grad = run_post(dk, back, w_query, w_key, w_value)
    return prefix_grad[None], latent_grad[None], key_wgrad


def solution(mesh):
    grid = Mesh(mesh.devices.reshape(4, 8, 2, 2, 2), ("y", "z", "x_high", "x_low", "core"))
    seq, dp = ("y", "z"), ("x_high", "x_low", "core")
    return jax.shard_map(
        on_device,
        mesh=grid,
        in_specs=(
            P(dp, seq, None),
            P(dp, seq, None),
            P(dp, seq, None),
            P(dp, seq, None),
            P(dp, None),
            P(),
            P(),
            P(),
        ),
        out_specs=(P(dp, seq, None), P(dp, seq, None), P(seq + dp, None)),
        check_vma=False,
    )
```
